512 devices in a mesh: row: 16 (over z, core), col: 32 (over x, y).
Axes of the slice: x: 4, y: 8, z: 8, core: 2. Of those that a mesh axis runs over, the one named last changes fastest.
Arguments:
- trail_adj: float32 [16384, 16384], P('row', 'col'), may hold values from -34 to 34
- factor_panels: float32 [16384, 384], P('row', 'col'), may hold values from -4 to 4, as said below
- factor_adj: float32 [16384, 384], P('row', 'col'), may hold values from -6 to 6
Outputs:
- panel_adj: float32 [16384, 384], P('row', 'col')
The draws below stay inside these ranges and needn't reach their ends.
Inputs may be any that keep to these rules, and one draw needn't show every extreme that they name: `factor_panels`: in column block k of 128 columns, rows above k * 128 are zero and rows k * 128 to k * 128 + 127 form a lower-triangular block with diagonal entries 1.5 to 4.
All inputs are finite; a program needn't handle non-finite values.
Results may differ from the reference program's by a relative error of at most 0.00011.
Values sent between devices are 32-bit elements; how exact they have to be, the bound alone decides.
No kernel may reach another device: no remote copies, remote signals or barrier semaphores. Data moves between devices by JAX's collectives and lax.ppermute only.
A program may use at most 64 MiB of HBM per device.

```python
import math
import jax
import jax.numpy as jnp
from jax import lax

B = 128
STEPS = 3
N = 16384
P_SIZE = 384


def draw_trail_adj(key, part):
    key = jax.random.fold_in(key, 11)
    noise_key = jax.random.fold_in(key, 0)
    values = jnp.clip(jax.random.normal(noise_key, (N, N), jnp.float32), -6.0, 6.0)
    return 0.70710678 * (values + values.T)


def draw_factor_panels(key, part):
    key = jax.random.fold_in(key, 12)
    noise_key, diag_key = jax.random.split(key)
    noise = jnp.clip(jax.random.normal(noise_key, (N, P_SIZE), jnp.float32), -6.0, 6.0)
    diagonal = jnp.exp(jax.random.uniform(diag_key, (N, P_SIZE), jnp.float32, math.log(1.5), math.log(4.0)))
    row_ids = jnp.arange(N, dtype=jnp.int32)[:, None]
    col_ids = jnp.arange(P_SIZE, dtype=jnp.int32)[None, :]
    block_start = col_ids // B * B
    in_block = (row_ids >= block_start) & (row_ids < block_start + B)
    below_block = row_ids >= block_start + B
    values = jnp.where(below_block, noise * N ** (-0.5), 0.0)
    values = jnp.where(in_block & (row_ids > col_ids), noise * B ** (-0.5), values)
    values = jnp.where(row_ids == col_ids, diagonal, values)
    return values.astype(jnp.float32)


def level_of(key, shape, pieces, least, largest):
    gain = 1.0
    for dim, parts in pieces:
        steps = jax.random.uniform(jax.random.fold_in(jax.random.fold_in(key, 6), dim), (parts,), jnp.float32, least / len(pieces), largest / len(pieces))
        gain = gain * jnp.repeat(jnp.exp(steps), shape[dim] // parts).reshape((-1,) + (1,) * (len(shape) - 1 - dim))
    return gain


def bell_draw(key, dims, width, reach, pieces=(), kind=jnp.bfloat16):
    values = width * jax.random.normal(key, dims, jnp.float32)
    if pieces:
        values = values * level_of(key, dims, pieces, -0.22, 0.18)
    return jnp.clip(values, -reach, reach).astype(kind)


def setup_inputs(seed: int = 0) -> dict:
    splits = jax.random.split(jax.random.key(seed), 4)
    trail_adj = draw_trail_adj(jax.random.fold_in(splits[3], 71), 0)
    factor_panels = draw_factor_panels(jax.random.fold_in(splits[3], 71), 0)
    factor_adj = bell_draw(splits[2], (N, P_SIZE), 1.0, 6.0, ((0, 16), (1, 32)), jnp.float32)
    return dict(trail_adj=trail_adj, factor_panels=factor_panels, factor_adj=factor_adj)


def mdot(operand, other):
    return jnp.dot(operand.astype(jnp.float32), other.astype(jnp.float32), precision=lax.Precision.HIGHEST, preferred_element_type=jnp.float32)

def place_rows(block_rows, global_rows, first_row, block_height):
    offsets = global_rows - first_row
    inside = (offsets >= 0) & (offsets < block_height)
    taken = jnp.take(block_rows, jnp.clip(offsets, 0, block_height - 1), axis=0)
    return jnp.where(inside[:, None], taken, jnp.zeros_like(taken))

def diag_adjoint(lower_block, lower_inverse, block_total):
    product = mdot(lower_block.T, block_total)
    halved = jnp.tril(product) - 0.5 * jnp.diag(jnp.diag(product))
    sandwich = mdot(mdot(lower_inverse.T, halved), lower_inverse)
    return 0.5 * (sandwich + sandwich.T)

def reference(trail_adj, factor_panels, factor_adj):
    total_rows = trail_adj.shape[0]
    panel_width = STEPS * B
    global_rows = jnp.arange(total_rows, dtype=jnp.int32)
    accum = jnp.zeros((total_rows, panel_width), jnp.float32)
    identity = jnp.eye(B, dtype=jnp.float32)
    for panel_step in reversed(range(STEPS)):
        col_start = panel_step * B
        lower_mask = (global_rows >= col_start + B)[:, None]
        column = jnp.where(lower_mask, factor_panels[:, col_start:col_start + B], 0.0)
        lower_block = jnp.tril(factor_panels[col_start:col_start + B, col_start:col_start + B])
        block_adj = factor_adj[col_start:col_start + B, col_start:col_start + B]
        lower_inverse = jax.scipy.linalg.solve_triangular(lower_block, identity, lower=True)
        image_term = mdot(trail_adj, column) + mdot(accum, column[:panel_width])
        image_term = image_term + place_rows(mdot(accum.T, column), global_rows, 0, panel_width)
        factor_grad = jnp.where(lower_mask, factor_adj[:, col_start:col_start + B] - 2.0 * image_term, 0.0)
        off_adj = mdot(factor_grad, lower_inverse)
        block_total = block_adj - mdot(column.T, off_adj)
        diag_adj = diag_adjoint(lower_block, lower_inverse, block_total)
        new_cols = jnp.where(lower_mask, 0.5 * off_adj, 0.0) + 0.5 * place_rows(diag_adj, global_rows, col_start, B)
        accum = accum.at[:, col_start:col_start + B].set(new_cols)
    return accum + place_rows(accum[:panel_width].T, global_rows, 0, panel_width)
```

```python
import functools

import jax
import jax.numpy as jnp
from jax import lax
from jax.experimental import pallas as pl
from jax.experimental.pallas import tpu as pltpu
from jax.sharding import PartitionSpec as P

B = 128
STEPS = 3
PW = STEPS * B
HI = lax.Precision.HIGHEST
X_SIZE, Y_SIZE = 4, 8
Y_GROUPS = [[x * Y_SIZE + y for y in range(Y_SIZE)] for x in range(X_SIZE)]
X_GROUPS = [[x * Y_SIZE + y for x in range(X_SIZE)] for y in range(Y_SIZE)]
PARAMS = pltpu.CompilerParams(vmem_limit_bytes=48 * 1024 * 1024)


def dot(a, b):
    return jnp.dot(a, b, precision=HI, preferred_element_type=jnp.float32)


def dot_nt(a, b):
    return lax.dot_general(
        a, b, (((1,), (1,)), ((), ())), precision=HI, preferred_element_type=jnp.float32
    )


def owner_col(row, half):
    return (2 * (row % 2) + half) * Y_SIZE + row // 2


def product_kernel(f_ref, t_ref, out_ref, ft_ref, acc_ref):
    row = lax.axis_index("row")
    panel = lax.broadcasted_iota(jnp.int32, (PW, B), 0) // B
    for b in range(8):
        part = f_ref[pl.ds(b, PW, stride=8), :]
        if b < STEPS:
            part = jnp.where((row > 0) | (panel < b), part, 0.0)
        ft_ref[:, b * B : (b + 1) * B] = part
    acc_ref[...] = dot(ft_ref[...], t_ref[...])
    for device in range(16):
        for half in range(2):
            first = 12 * owner_col(device, half)
            for b in range(4):
                out_ref[pl.ds(device * 96 + half * 48 + b, 12, stride=4), :] = acc_ref[
                    first : first + 12, b * B : (b + 1) * B
                ]


def sum_kernel(s_ref, a_ref, b_ref):
    odd = lax.axis_index("col") % 2 == 1
    low = jnp.sum(s_ref[:, 0:48, :], axis=0)
    high = jnp.sum(s_ref[:, 48:96, :], axis=0)
    a_ref[...] = jnp.where(odd, high, low)
    b_ref[...] = jnp.where(odd, low, high)


def inverse_kernel(f_ref, l_ref, lt_ref, li_ref, lit_ref, litp_ref):
    @pl.when(lax.axis_index("row") == 0)
    def _():
        rows = lax.broadcasted_iota(jnp.int32, (B, B), 0)
        cols = lax.broadcasted_iota(jnp.int32, (B, B), 1)
        for b in range(STEPS):
            lt_ref[:, b * B : (b + 1) * B] = f_ref[pl.ds(b, PW, stride=8), :]
        zero = jnp.zeros((B, B), jnp.float32)

        def blk(i, j):
            return (slice(i * B, (i + 1) * B), slice(j * B, (j + 1) * B))

        lt = {}
        for i in range(STEPS):
            for j in range(STEPS):
                if i > j:
                    lt_ref[blk(i, j)] = zero
                    continue
                value = lt_ref[blk(i, j)]
                if i == j:
                    value = jnp.where(rows <= cols, value, 0.0)
                    lt_ref[blk(i, j)] = value
                lt[i, j] = value
        inv = {}
        for i in range(STEPS):
            inv[i, i] = jnp.where(rows == cols, 1.0 / lt[i, i], 0.0)
        size = 1
        while size < B:
            mask = (rows // (2 * size) == cols // (2 * size)) & (rows // size < cols // size)
            step = [dot(inv[i, i], jnp.where(mask, lt[i, i], 0.0)) for i in range(STEPS)]
            for i in range(STEPS):
                inv[i, i] = inv[i, i] - dot(step[i], inv[i, i])
            size *= 2
        inv[0, 1] = -dot(dot(inv[0, 0], lt[0, 1]), inv[1, 1])
        inv[1, 2] = -dot(dot(inv[1, 1], lt[1, 2]), inv[2, 2])
        inv[0, 2] = -dot(dot(inv[0, 0], lt[0, 2]) + dot(inv[0, 1], lt[1, 2]), inv[2, 2])
        for i in range(STEPS):
            for j in range(STEPS):
                value = inv.get((i, j), zero)
                lit_ref[blk(i, j)] = value
                litp_ref[pl.ds(4 * i * B + j, B, stride=4), :] = value
                li_ref[blk(j, i)] = value.T if (i, j) in inv else zero
                l_ref[blk(j, i)] = lt[i, j].T if (i, j) in lt else zero
            litp_ref[pl.ds(4 * i * B + 3, B, stride=4), :] = zero


def gram_kernel(ra_ref, rb_ref, g_ref, ft_ref, litp_ref, pay_ref, y_ref, half_ref, ym_ref):
    row, col = lax.axis_index("row"), lax.axis_index("col")
    first = (col // Y_SIZE) % 2 == 0
    ra, rb = ra_ref[...], rb_ref[...]
    half_ref[0:48, :] = jnp.where(first, ra, rb)
    half_ref[48:96, :] = jnp.where(first, rb, ra)
    panel = (12 * col + lax.broadcasted_iota(jnp.int32, (12, B), 0)) // B
    top, diag = [], jnp.zeros((12, B), jnp.float32)
    for b in range(8):
        g = g_ref[pl.ds(b, 12, stride=8), :]
        y = g - 2.0 * half_ref[pl.ds(b // 4 * 48 + b % 4, 12, stride=4), :]
        y_ref[pl.ds(b, 12, stride=8), :] = y
        if b < STEPS:
            top.append(y)
            diag = jnp.where(panel == b, g, diag)
            y = jnp.where(row > 0, y, 0.0)
        ym_ref[:, b * B : (b + 1) * B] = y
    gram = dot_nt(ym_ref[...], ft_ref[...])
    for k in range(STEPS):
        below = jnp.where(row == 0, top[k], 0.0)
        pay_ref[pl.ds(k, 12, stride=4), :] = jnp.where(
            panel >= k, gram[:, k * B : (k + 1) * B], below
        )
    pay_ref[pl.ds(3, 12, stride=4), :] = jnp.where(row == 0, diag, 0.0)
    pay_ref[48:96, :] = litp_ref[pl.ds(pl.multiple_of(48 * col, 16), 48), :]


def tail_kernel(
    w_ref, own_ref, l_ref, lt_ref, li_ref, lit_ref, out_ref, yt_ref, own2_ref, u_ref, wp_ref, cut_ref
):
    row, col = lax.axis_index("row"), lax.axis_index("col")
    for x in range(X_SIZE):
        for b in range(8):
            yt_ref[96 * x : 96 * (x + 1), b * B : (b + 1) * B] = w_ref[
                pl.ds(x * 1152 + 384 + b, 96, stride=8), :
            ]
    for k in range(STEPS):
        own2_ref[:, k * B : (k + 1) * B] = own_ref[pl.ds(k, 12, stride=4), :]
    out_ref[...] = 0.5 * dot(own2_ref[...], yt_ref[...])

    @pl.when(row == 0)
    def _():
        for x in range(X_SIZE):
            for k in range(4):
                u_ref[96 * x : 96 * (x + 1), k * B : (k + 1) * B] = w_ref[
                    pl.ds(x * 1152 + k, 96, stride=4), :
                ]
        rows = lax.broadcasted_iota(jnp.int32, (B, B), 0)
        cols = lax.broadcasted_iota(jnp.int32, (B, B), 1)

        def blk(i, j):
            return (slice(i * B, (i + 1) * B), slice(j * B, (j + 1) * B))

        def low(i, j):
            return l_ref[blk(i, j)]

        wide = lax.broadcasted_iota(jnp.int32, (PW, PW), 0) // B
        tall = lax.broadcasted_iota(jnp.int32, (PW, PW), 1) // B
        zt = jnp.where(wide >= tall, u_ref[:, 0:PW], 0.0)
        yt_ref[:, 0:PW] = dot(lit_ref[...], zt)

        def vt(j, k):
            return yt_ref[blk(j, k)]

        def y_of(j, k):
            return u_ref[blk(k, j)].T

        def g_of(k):
            return u_ref[blk(k, STEPS)]

        def diag_adjoint(k, total_t):
            product_t = dot(total_t, low(k, k))
            halved_t = jnp.where(rows < cols, product_t, jnp.where(rows == cols, 0.5 * product_t, 0.0))
            sandwich = dot(dot(lit_ref[blk(k, k)], halved_t), li_ref[blk(k, k)])
            return 0.5 * (sandwich + sandwich.T)

        diag2 = diag_adjoint(2, g_of(2) - vt(2, 2))
        off21 = dot(y_of(2, 1) - 2.0 * dot(diag2, low(2, 1)) - vt(2, 1), li_ref[blk(1, 1)])
        off12 = off21.T
        diag1 = diag_adjoint(1, g_of(1) - vt(1, 1) - dot(off12, low(2, 1)))
        off20 = dot(
            y_of(2, 0) - dot(off21, low(1, 0)) - 2.0 * dot(diag2, low(2, 0)) - vt(2, 0),
            li_ref[blk(0, 0)],
        )
        off10 = dot(
            y_of(1, 0) - 2.0 * dot(diag1, low(1, 0)) - dot(off12, low(2, 0)) - vt(1, 0),
            li_ref[blk(0, 0)],
        )
        off02, off01 = off20.T, off10.T
        diag0 = diag_adjoint(0, g_of(0) - vt(0, 0) - dot(off01, low(1, 0)) - dot(off02, low(2, 0)))
        whole = {
            (0, 0): diag0, (1, 1): diag1, (2, 2): diag2,
            (1, 0): 0.5 * off10, (2, 0): 0.5 * off20, (2, 1): 0.5 * off21,
            (0, 1): 0.5 * off01, (0, 2): 0.5 * off02, (1, 2): 0.5 * off12,
        }
        for i in range(STEPS):
            for j in range(STEPS):
                wp_ref[pl.ds(4 * i * B + j, B, stride=4), :] = whole[i, j]
        cut_ref[...] = wp_ref[pl.ds(pl.multiple_of(48 * col, 16), 48), :]
        for k in range(STEPS):
            out_ref[:, k * B : (k + 1) * B] = cut_ref[pl.ds(k, 12, stride=4), :]


def f32(*shape):
    return jax.ShapeDtypeStruct(shape, jnp.float32)


def vmem(*shape):
    return pltpu.VMEM(shape, jnp.float32)


def call(kernel, out_shape, *args, scratch=(), flops=0):
    many = isinstance(out_shape, (list, tuple))
    spec = pl.BlockSpec(memory_space=pltpu.VMEM)
    total = sum(a.size for a in args) * 4
    return pl.pallas_call(
        kernel,
        out_shape=out_shape,
        in_specs=[spec] * len(args),
        out_specs=[spec] * len(out_shape) if many else spec,
        scratch_shapes=list(scratch),
        compiler_params=PARAMS,
        cost_estimate=pl.CostEstimate(flops=flops, bytes_accessed=total, transcendentals=0),
    )(*args)


def spread(value, groups):
    count = len(groups[0])
    copies = jnp.broadcast_to(value[None], (count,) + value.shape)
    return lax.all_to_all(copies, "col", 0, 0, axis_index_groups=groups)


def on_device(trail_adj, factor_panels, factor_adj):
    factor = factor_panels.T.reshape(96, B)
    adjoint = factor_adj.T.reshape(96, B)
    near = spread(factor, Y_GROUPS).reshape(Y_SIZE * 96, B)
    panels = spread(near, X_GROUPS).reshape(PW * 8, B)
    partial, ft = call(
        product_kernel, [f32(1536, B), f32(PW, 1024)], panels, trail_adj,
        scratch=[vmem(PW, 512)], flops=12 * 1024 * 512 * PW,
    )
    pieces = lax.all_to_all(partial.reshape(16, 96, B), "row", 0, 0)
    send_a, send_b = call(sum_kernel, [f32(48, B), f32(48, B)], pieces)
    rows, cols = range(16), range(32)
    to_a = [(r * 32 + c, c // 2 * 32 + owner_col(r, c % 2)) for r in rows for c in cols]
    to_b = [(r * 32 + c, c // 2 * 32 + owner_col(r, 1 - c % 2)) for r in rows for c in cols]
    got_a = lax.ppermute(send_a, ("row", "col"), to_a)
    got_b = lax.ppermute(send_b, ("row", "col"), to_b)
    low, low_t, inv, inv_t, inv_tp = call(
        inverse_kernel, [f32(PW, PW)] * 4 + [f32(1536, B)], panels, flops=12 * 60 * B**3,
    )
    payload, own_y = call(
        gram_kernel, [f32(96, B), f32(96, B)], got_a, got_b, adjoint, ft, inv_tp,
        scratch=[vmem(96, B), vmem(12, 1024)], flops=12 * 12 * 1024 * PW,
    )
    all_pay = lax.all_gather(payload, "row", axis=0)
    corner = jnp.sum(all_pay[:, :48], axis=0)
    own = all_pay[0, 48:]
    near = spread(jnp.concatenate([corner, own_y], axis=0), Y_GROUPS)
    near = jnp.concatenate([near[:, :48].reshape(384, B), near[:, 48:].reshape(768, B)], axis=0)
    whole = spread(near, X_GROUPS).reshape(X_SIZE * 1152, B)
    out = call(
        tail_kernel, f32(12, 1024), whole, own, low, low_t, inv, inv_t,
        scratch=[vmem(PW, 1024), vmem(12, PW), vmem(PW, 512), vmem(1536, B), vmem(48, B)],
        flops=12 * 12 * 1024 * PW,
    )
    return out.T


def solution(mesh):
    in_specs = (P("row", "col"), P("row", "col"), P("row", "col"))
    out_specs = P("row", "col")
    return jax.shard_map(
        on_device, mesh=mesh, in_specs=in_specs, out_specs=out_specs, check_vma=False
    )
```

```python
import functools

import jax
import jax.numpy as jnp
from jax import lax
from jax.experimental import pallas as pl
from jax.experimental.pallas import tpu as pltpu
from jax.sharding import PartitionSpec as P

B = 128
STEPS = 3
PW = STEPS * B
HI = lax.Precision.HIGHEST
X_SIZE, Y_SIZE = 4, 8
Y_GROUPS = [[x * Y_SIZE + y for y in range(Y_SIZE)] for x in range(X_SIZE)]
X_GROUPS = [[x * Y_SIZE + y for x in range(X_SIZE)] for y in range(Y_SIZE)]
Z_GROUPS = [[2 * z + core for z in range(8)] for core in range(2)]
PARAMS = pltpu.CompilerParams(vmem_limit_bytes=48 * 1024 * 1024)


def dot(a, b):
    return jnp.dot(a, b, precision=HI, preferred_element_type=jnp.float32)


def dot_nt(a, b):
    return lax.dot_general(
        a, b, (((1,), (1,)), ((), ())), precision=HI, preferred_element_type=jnp.float32
    )


def place(row, col, half):
    x, y = col // Y_SIZE, col % Y_SIZE
    x_to, y_to = (x + 2 * (row % 2) + half) % X_SIZE, (y + row // 2) % Y_SIZE
    return col // 2 * (X_SIZE * Y_SIZE) + x_to * Y_SIZE + y_to


def product_kernel(f_ref, t_ref, send_ref, keep_ref, ft_ref, top_ref, acc_ref, cut_ref, pick_ref):
    row, col = lax.axis_index("row"), lax.axis_index("col")
    x, y = col // Y_SIZE, col % Y_SIZE
    panel = lax.broadcasted_iota(jnp.int32, (PW, B), 0) // B
    for b in range(8):
        part = f_ref[pl.ds(b, PW, stride=8), :]
        if b < STEPS:
            top_ref[:, b * B : (b + 1) * B] = part
            part = jnp.where((row > 0) | (panel < b), part, 0.0)
        ft_ref[:, b * B : (b + 1) * B] = part
    for core, target in ((1 - row % 2, send_ref), (row % 2, keep_ref)):
        for half in range(2):
            first = pl.multiple_of((x + 2 * core + half) % X_SIZE * 96, 8)
            pick_ref[half * 96 : (half + 1) * 96, :] = ft_ref[pl.ds(first, 96), :]
        acc_ref[...] = dot(pick_ref[...], t_ref[...])
        for b in range(4):
            cut_ref[pl.ds(b, PW // 2, stride=4), :] = acc_ref[:, b * B : (b + 1) * B]
        for z in range(8):
            for half in range(2):
                first = pl.multiple_of(half * 384 + (y + z) % Y_SIZE * 48, 16)
                target[z * 96 + half * 48 : z * 96 + half * 48 + 48, :] = cut_ref[pl.ds(first, 48), :]


def sum_kernel(s_ref, a_ref, b_ref):
    odd = lax.axis_index("col") % 2 == 1
    low = jnp.sum(s_ref[:, 0:48, :], axis=0)
    high = jnp.sum(s_ref[:, 48:96, :], axis=0)
    a_ref[...] = jnp.where(odd, high, low)
    b_ref[...] = jnp.where(odd, low, high)


def corner_block(kind, i, j):
    lower = {(0, 0): 0, (1, 0): 1, (1, 1): 2, (2, 0): 3, (2, 1): 4, (2, 2): 5}
    if kind == "l":
        place = lower[i, j]
    elif kind == "lit":
        place = 6 + lower[j, i]
    else:
        place = 12 + i
    return slice(place * B, (place + 1) * B)


def inverse_kernel(top_ref, fac_ref, litp_ref):
    @pl.when(lax.axis_index("row") == 0)
    def _():
        rows = lax.broadcasted_iota(jnp.int32, (B, B), 0)
        cols = lax.broadcasted_iota(jnp.int32, (B, B), 1)
        lt = {}
        for j in range(STEPS):
            for i in range(j + 1):
                value = top_ref[i * B : (i + 1) * B, j * B : (j + 1) * B]
                lt[i, j] = jnp.where(rows <= cols, value, 0.0) if i == j else value
                fac_ref[corner_block("l", j, i)] = lt[i, j].T
        inv = {}
        for i in range(STEPS):
            inv[i, i] = jnp.where(rows == cols, 1.0 / lt[i, i], 0.0)
        size = 1
        while size < B:
            mask = (rows // (2 * size) == cols // (2 * size)) & (rows // size < cols // size)
            step = [dot(inv[i, i], jnp.where(mask, lt[i, i], 0.0)) for i in range(STEPS)]
            for i in range(STEPS):
                inv[i, i] = inv[i, i] - dot(step[i], inv[i, i])
            size *= 2
        inv[0, 1] = -dot(dot(inv[0, 0], lt[0, 1]), inv[1, 1])
        inv[1, 2] = -dot(dot(inv[1, 1], lt[1, 2]), inv[2, 2])
        inv[0, 2] = -dot(dot(inv[0, 0], lt[0, 2]) + dot(inv[0, 1], lt[1, 2]), inv[2, 2])
        zero = jnp.zeros((B, B), jnp.float32)
        for i in range(STEPS):
            for j in range(4):
                litp_ref[pl.ds(4 * i * B + j, B, stride=4), :] = inv.get((i, j), zero)
            for j in range(i, STEPS):
                fac_ref[corner_block("lit", i, j)] = inv[i, j]
            fac_ref[corner_block("li", i, i)] = inv[i, i].T


def gram_kernel(ra_ref, rb_ref, g_ref, ft_ref, litp_ref, pay_ref, y_ref, half_ref, ym_ref):
    row, col = lax.axis_index("row"), lax.axis_index("col")
    first = (col // Y_SIZE + row // 4) % 2 == 0
    ra, rb = ra_ref[...], rb_ref[...]
    half_ref[0:48, :] = jnp.where(first, ra, rb)
    half_ref[48:96, :] = jnp.where(first, rb, ra)
    panel = (12 * col + lax.broadcasted_iota(jnp.int32, (12, B), 0)) // B
    top, diag = [], jnp.zeros((12, B), jnp.float32)
    for b in range(8):
        g = g_ref[pl.ds(b, 12, stride=8), :]
        y = g - 2.0 * half_ref[pl.ds(b // 4 * 48 + b % 4, 12, stride=4), :]
        y_ref[pl.ds(b, 12, stride=8), :] = y
        if b < STEPS:
            top.append(y)
            diag = jnp.where(panel == b, g, diag)
            y = jnp.where(row > 0, y, 0.0)
        ym_ref[:, b * B : (b + 1) * B] = y
    gram = dot_nt(ym_ref[...], ft_ref[...])
    for k in range(STEPS):
        below = jnp.where(row == 0, top[k], 0.0)
        pay_ref[pl.ds(k, 12, stride=4), :] = jnp.where(
            panel >= k, gram[:, k * B : (k + 1) * B], below
        )
    pay_ref[pl.ds(3, 12, stride=4), :] = jnp.where(row == 0, diag, 0.0)
    own = litp_ref[pl.ds(pl.multiple_of(48 * col, 16), 48), :]
    pay_ref[48:96, :] = jnp.where(row == 0, own, 0.0)


def tail_kernel(
    y0_ref, y1_ref, y2_ref, y3_ref, mine_ref, got_ref, w_ref, fac_ref,
    out_ref, yt_ref, own_ref, lit_ref, u_ref, vt_ref, wp_ref, cut_ref,
):
    row = lax.axis_index("row")
    x = lax.axis_index("col") // Y_SIZE
    for step, y_ref in enumerate((y0_ref, y1_ref, y2_ref, y3_ref)):
        first = pl.multiple_of((x + step) % X_SIZE * 96, 8)
        for b in range(8):
            yt_ref[pl.ds(first, 96), b * B : (b + 1) * B] = y_ref[pl.ds(b, 96, stride=8), :]
    own_ref[...] = jnp.where(row < 2, mine_ref[...], got_ref[0])
    for k in range(STEPS):
        lit_ref[:, k * B : (k + 1) * B] = own_ref[pl.ds(k, 12, stride=4), :]
    out_ref[...] = 0.5 * dot(lit_ref[...], yt_ref[...])

    @pl.when(row == 0)
    def _():
        for k in range(4):
            u_ref[:, k * B : (k + 1) * B] = w_ref[pl.ds(k, PW, stride=4), :]
        rows = lax.broadcasted_iota(jnp.int32, (B, B), 0)
        cols = lax.broadcasted_iota(jnp.int32, (B, B), 1)

        def blk(i, j):
            return (slice(i * B, (i + 1) * B), slice(j * B, (j + 1) * B))

        def fac(kind, i, j):
            return fac_ref[corner_block(kind, i, j)]

        for j in range(STEPS):
            for k in range(j + 1):
                terms = [dot(fac("lit", j, i), u_ref[blk(i, k)]) for i in range(j, STEPS)]
                vt_ref[blk(j, k)] = functools.reduce(jnp.add, terms)

        def vt(j, k):
            return vt_ref[blk(j, k)]

        def y_of(j, k):
            return u_ref[blk(k, j)].T

        def g_of(k):
            return u_ref[blk(k, STEPS)]

        def diag_adjoint(k, total_t):
            product_t = dot(total_t, fac("l", k, k))
            halved_t = jnp.where(rows < cols, product_t, jnp.where(rows == cols, 0.5 * product_t, 0.0))
            sandwich = dot(dot(fac("lit", k, k), halved_t), fac("li", k, k))
            return 0.5 * (sandwich + sandwich.T)

        l10, l20, l21 = fac("l", 1, 0), fac("l", 2, 0), fac("l", 2, 1)
        li0, li1 = fac("li", 0, 0), fac("li", 1, 1)
        diag2 = diag_adjoint(2, g_of(2) - vt(2, 2))
        off21 = dot(y_of(2, 1) - 2.0 * dot(diag2, l21) - vt(2, 1), li1)
        off12 = off21.T
        diag1 = diag_adjoint(1, g_of(1) - vt(1, 1) - dot(off12, l21))
        off20 = dot(y_of(2, 0) - dot(off21, l10) - 2.0 * dot(diag2, l20) - vt(2, 0), li0)
        off10 = dot(y_of(1, 0) - 2.0 * dot(diag1, l10) - dot(off12, l20) - vt(1, 0), li0)
        off02, off01 = off20.T, off10.T
        diag0 = diag_adjoint(0, g_of(0) - vt(0, 0) - dot(off01, l10) - dot(off02, l20))
        whole = {
            (0, 0): diag0, (1, 1): diag1, (2, 2): diag2,
            (1, 0): 0.5 * off10, (2, 0): 0.5 * off20, (2, 1): 0.5 * off21,
            (0, 1): 0.5 * off01, (0, 2): 0.5 * off02, (1, 2): 0.5 * off12,
        }
        for i in range(STEPS):
            for j in range(STEPS):
                wp_ref[pl.ds(4 * i * B + j, B, stride=4), :] = whole[i, j]
        start = pl.multiple_of(48 * lax.axis_index("col"), 16)
        cut_ref[...] = wp_ref[pl.ds(start, 48), :]
        for k in range(STEPS):
            out_ref[:, k * B : (k + 1) * B] = cut_ref[pl.ds(k, 12, stride=4), :]


def route_kernel(mine_ref, other_ref, _, out_ref, sum_ref, own_ref):
    mine, other = mine_ref[...], other_ref[...]
    corner = mine[0:48] + other[0:48]
    inverse = mine[48:96] + other[48:96]
    sum_ref[...] = corner
    own_ref[...] = inverse
    out_ref[0] = corner
    for z in range(1, 8):
        out_ref[z] = inverse


def corner_sum_kernel(mine_ref, got_ref, *rest):
    rest[-1][...] = mine_ref[...] + jnp.sum(got_ref[1:], axis=0)


def f32(*shape):
    return jax.ShapeDtypeStruct(shape, jnp.float32)


def vmem(*shape):
    return pltpu.VMEM(shape, jnp.float32)


def call(kernel, out_shape, *args, scratch=(), flops=0, after=()):
    many = isinstance(out_shape, (list, tuple))
    spec = pl.BlockSpec(memory_space=pltpu.VMEM)
    total = sum(a.size for a in args) * 4
    return pl.pallas_call(
        kernel,
        out_shape=out_shape,
        in_specs=[spec] * len(args) + [pl.BlockSpec(memory_space=pl.ANY)] * len(after),
        out_specs=[spec] * len(out_shape) if many else spec,
        scratch_shapes=list(scratch),
        compiler_params=PARAMS,
        cost_estimate=pl.CostEstimate(flops=flops, bytes_accessed=total, transcendentals=0),
    )(*args, *after)


def spread(value, axis, groups):
    count = len(groups[0])
    copies = jnp.broadcast_to(value[None], (count,) + value.shape)
    return lax.all_to_all(copies, axis, 0, 0, axis_index_groups=groups)


def between_cores(value):
    return lax.ppermute(value, "row", [(r, r ^ 1) for r in range(16)])


def from_x(value, step):
    pairs = [((c + step * Y_SIZE) % (X_SIZE * Y_SIZE), c) for c in range(X_SIZE * Y_SIZE)]
    return lax.ppermute(value, "col", pairs)


def on_device(trail_adj, factor_panels, factor_adj):
    factor = factor_panels.T.reshape(96, B)
    adjoint = factor_adj.T.reshape(96, B)
    near = spread(factor, "col", Y_GROUPS).reshape(Y_SIZE * 96, B)
    panels = spread(near, "col", X_GROUPS).reshape(PW * 8, B)
    send, keep, ft, ft_corner = call(
        product_kernel, [f32(768, B), f32(768, B), f32(PW, 1024), f32(PW, PW)], panels, trail_adj,
        scratch=[vmem(PW // 2, 512), vmem(768, B), vmem(PW // 2, 1024)], flops=12 * 1024 * 512 * PW,
    )
    both = (keep + between_cores(send)).reshape(8, 96, B)
    pieces = lax.all_to_all(both, "row", 0, 0, axis_index_groups=Z_GROUPS)
    send_a, send_b = call(sum_kernel, [f32(48, B), f32(48, B)], pieces)
    devices = [(r, c) for r in range(16) for c in range(32)]
    to_a = [(r * 32 + c, place(r, c, c % 2)) for r, c in devices]
    to_b = [(r * 32 + c, place(r, c, 1 - c % 2)) for r, c in devices]
    got_a = lax.ppermute(send_a, ("row", "col"), to_a)
    got_b = lax.ppermute(send_b, ("row", "col"), to_b)
    fac, inv_tp = call(
        inverse_kernel, [f32(15 * B, B), f32(1536, B)], ft_corner, flops=12 * 60 * B**3,
    )
    payload, own_y = call(
        gram_kernel, [f32(96, B), f32(96, B)], got_a, got_b, adjoint, ft, inv_tp,
        scratch=[vmem(96, B), vmem(12, 1024)], flops=12 * 12 * 1024 * PW,
    )
    near_y = spread(own_y, "col", Y_GROUPS).reshape(Y_SIZE * 96, B)
    all_y = [near_y] + [from_x(near_y, step) for step in range(1, X_SIZE)]
    out_u, sum_u, own = call(
        route_kernel, [f32(8, 48, B), f32(48, B), f32(48, B)], payload, between_cores(payload),
        after=[near_y],
    )
    got = lax.all_to_all(out_u, "row", 0, 0, axis_index_groups=Z_GROUPS)
    corner_u = call(corner_sum_kernel, f32(48, B), sum_u, got, after=all_y[1:])
    near_u = spread(corner_u, "col", Y_GROUPS).reshape(Y_SIZE * 48, B)
    all_u = spread(near_u, "col", X_GROUPS).reshape(PW * 4, B)
    out = call(
        tail_kernel, f32(12, 1024), *all_y, own, got, all_u, fac,
        scratch=[
            vmem(PW, 1024), vmem(48, B), vmem(12, PW), vmem(PW, 512), vmem(PW, PW), vmem(1536, B),
            vmem(48, B),
        ],
        flops=12 * 12 * 1024 * PW,
    )
    return out.T


def solution(mesh):
    in_specs = (P("row", "col"), P("row", "col"), P("row", "col"))
    out_specs = P("row", "col")
    return jax.shard_map(
        on_device, mesh=mesh, in_specs=in_specs, out_specs=out_specs, check_vma=False
    )
```

```python
import functools

import jax
import jax.numpy as jnp
from jax import lax
from jax.experimental import pallas as pl
from jax.experimental.pallas import tpu as pltpu
from jax.sharding import PartitionSpec as P

B = 128
STEPS = 3
PW = STEPS * B
HI = lax.Precision.HIGHEST
X_SIZE, Y_SIZE = 4, 8
Y_GROUPS = [[x * Y_SIZE + y for y in range(Y_SIZE)] for x in range(X_SIZE)]
X_GROUPS = [[x * Y_SIZE + y for x in range(X_SIZE)] for y in range(Y_SIZE)]
Z_GROUPS = [[2 * z + core for z in range(8)] for core in range(2)]
PARAMS = pltpu.CompilerParams(vmem_limit_bytes=48 * 1024 * 1024)


def dot(a, b):
    return jnp.dot(a, b, precision=HI, preferred_element_type=jnp.float32)


def dot_nt(a, b):
    return lax.dot_general(
        a, b, (((1,), (1,)), ((), ())), precision=HI, preferred_element_type=jnp.float32
    )


def place(row, col, half):
    x, y = col // Y_SIZE, col % Y_SIZE
    x_to, y_to = (x + 2 * (row % 2) + half) % X_SIZE, (y + row // 2) % Y_SIZE
    return col // 2 * (X_SIZE * Y_SIZE) + x_to * Y_SIZE + y_to


def product_kernel(f_ref, t_ref, send_ref, keep_ref, ft_ref, top_ref, acc_ref, cut_ref):
    row, col = lax.axis_index("row"), lax.axis_index("col")
    x, y = col // Y_SIZE, col % Y_SIZE
    panel = lax.broadcasted_iota(jnp.int32, (PW, B), 0) // B
    for b in range(8):
        part = f_ref[pl.ds(b, PW, stride=8), :]
        if b < STEPS:
            top_ref[:, b * B : (b + 1) * B] = part
            part = jnp.where((row > 0) | (panel < b), part, 0.0)
        ft_ref[:, b * B : (b + 1) * B] = part
    acc_ref[...] = dot(ft_ref[...], t_ref[...])
    for b in range(4):
        cut_ref[pl.ds(b, PW, stride=4), :] = acc_ref[:, b * B : (b + 1) * B]
    for core, target in ((1 - row % 2, send_ref), (row % 2, keep_ref)):
        for z in range(8):
            for half in range(2):
                x_to, y_to = (x + 2 * core + half) % X_SIZE, (y + z) % Y_SIZE
                first = pl.multiple_of((x_to * Y_SIZE + y_to) * 48, 16)
                target[z * 96 + half * 48 : z * 96 + half * 48 + 48, :] = cut_ref[pl.ds(first, 48), :]


def sum_kernel(s_ref, a_ref, b_ref):
    odd = lax.axis_index("col") % 2 == 1
    low = jnp.sum(s_ref[:, 0:48, :], axis=0)
    high = jnp.sum(s_ref[:, 48:96, :], axis=0)
    a_ref[...] = jnp.where(odd, high, low)
    b_ref[...] = jnp.where(odd, low, high)


def corner_block(kind, i, j):
    lower = {(0, 0): 0, (1, 0): 1, (1, 1): 2, (2, 0): 3, (2, 1): 4, (2, 2): 5}
    if kind == "l":
        place = lower[i, j]
    elif kind == "lit":
        place = 6 + lower[j, i]
    else:
        place = 12 + i
    return slice(place * B, (place + 1) * B)


def inverse_kernel(top_ref, fac_ref, litp_ref):
    @pl.when(lax.axis_index("row") == 0)
    def _():
        rows = lax.broadcasted_iota(jnp.int32, (B, B), 0)
        cols = lax.broadcasted_iota(jnp.int32, (B, B), 1)
        lt = {}
        for j in range(STEPS):
            for i in range(j + 1):
                value = top_ref[i * B : (i + 1) * B, j * B : (j + 1) * B]
                lt[i, j] = jnp.where(rows <= cols, value, 0.0) if i == j else value
                fac_ref[corner_block("l", j, i)] = lt[i, j].T
        inv = {}
        for i in range(STEPS):
            inv[i, i] = jnp.where(rows == cols, 1.0 / lt[i, i], 0.0)
        size = 1
        while size < B:
            mask = (rows // (2 * size) == cols // (2 * size)) & (rows // size < cols // size)
            step = [dot(inv[i, i], jnp.where(mask, lt[i, i], 0.0)) for i in range(STEPS)]
            for i in range(STEPS):
                inv[i, i] = inv[i, i] - dot(step[i], inv[i, i])
            size *= 2
        inv[0, 1] = -dot(dot(inv[0, 0], lt[0, 1]), inv[1, 1])
        inv[1, 2] = -dot(dot(inv[1, 1], lt[1, 2]), inv[2, 2])
        inv[0, 2] = -dot(dot(inv[0, 0], lt[0, 2]) + dot(inv[0, 1], lt[1, 2]), inv[2, 2])
        zero = jnp.zeros((B, B), jnp.float32)
        for i in range(STEPS):
            for j in range(4):
                litp_ref[pl.ds(4 * i * B + j, B, stride=4), :] = inv.get((i, j), zero)
            for j in range(i, STEPS):
                fac_ref[corner_block("lit", i, j)] = inv[i, j]
            fac_ref[corner_block("li", i, i)] = inv[i, i].T


def gram_kernel(ra_ref, rb_ref, g_ref, ft_ref, litp_ref, pay_ref, y_ref, half_ref, ym_ref):
    row, col = lax.axis_index("row"), lax.axis_index("col")
    first = (col // Y_SIZE + row // 4) % 2 == 0
    ra, rb = ra_ref[...], rb_ref[...]
    half_ref[0:48, :] = jnp.where(first, ra, rb)
    half_ref[48:96, :] = jnp.where(first, rb, ra)
    panel = (12 * col + lax.broadcasted_iota(jnp.int32, (12, B), 0)) // B
    top, diag = [], jnp.zeros((12, B), jnp.float32)
    for b in range(8):
        g = g_ref[pl.ds(b, 12, stride=8), :]
        y = g - 2.0 * half_ref[pl.ds(b // 4 * 48 + b % 4, 12, stride=4), :]
        y_ref[b, 0:12, :] = y
        y_ref[b, 12:16, :] = jnp.zeros((4, B), jnp.float32)
        if b < STEPS:
            top.append(y)
            diag = jnp.where(panel == b, g, diag)
            y = jnp.where(row > 0, y, 0.0)
        ym_ref[:, b * B : (b + 1) * B] = y
    gram = dot_nt(ym_ref[...], ft_ref[...])
    for k in range(STEPS):
        below = jnp.where(row == 0, top[k], 0.0)
        pay_ref[pl.ds(k, 12, stride=4), :] = jnp.where(
            panel >= k, gram[:, k * B : (k + 1) * B], below
        )
    pay_ref[pl.ds(3, 12, stride=4), :] = jnp.where(row == 0, diag, 0.0)
    own = litp_ref[pl.ds(pl.multiple_of(48 * col, 16), 48), :]
    pay_ref[48:96, :] = jnp.where(row == 0, own, 0.0)


def corner_kernel(w_ref, fac_ref, out_ref, u_ref, vt_ref, wp_ref, cut_ref):
    @pl.when(lax.axis_index("row") == 0)
    def _():
        for x in range(X_SIZE):
            for k in range(4):
                u_ref[96 * x : 96 * (x + 1), k * B : (k + 1) * B] = w_ref[
                    pl.ds(480 * x + k, 96, stride=4), :
                ]
        rows = lax.broadcasted_iota(jnp.int32, (B, B), 0)
        cols = lax.broadcasted_iota(jnp.int32, (B, B), 1)

        def blk(i, j):
            return (slice(i * B, (i + 1) * B), slice(j * B, (j + 1) * B))

        def fac(kind, i, j):
            return fac_ref[corner_block(kind, i, j)]

        for j in range(STEPS):
            for k in range(j + 1):
                terms = [dot(fac("lit", j, i), u_ref[blk(i, k)]) for i in range(j, STEPS)]
                vt_ref[blk(j, k)] = functools.reduce(jnp.add, terms)

        def vt(j, k):
            return vt_ref[blk(j, k)]

        def y_of(j, k):
            return u_ref[blk(k, j)].T

        def g_of(k):
            return u_ref[blk(k, STEPS)]

        def diag_adjoint(k, total_t):
            product_t = dot(total_t, fac("l", k, k))
            halved_t = jnp.where(rows < cols, product_t, jnp.where(rows == cols, 0.5 * product_t, 0.0))
            sandwich = dot(dot(fac("lit", k, k), halved_t), fac("li", k, k))
            return 0.5 * (sandwich + sandwich.T)

        l10, l20, l21 = fac("l", 1, 0), fac("l", 2, 0), fac("l", 2, 1)
        li0, li1 = fac("li", 0, 0), fac("li", 1, 1)
        diag2 = diag_adjoint(2, g_of(2) - vt(2, 2))
        off21 = dot(y_of(2, 1) - 2.0 * dot(diag2, l21) - vt(2, 1), li1)
        off12 = off21.T
        diag1 = diag_adjoint(1, g_of(1) - vt(1, 1) - dot(off12, l21))
        off20 = dot(y_of(2, 0) - dot(off21, l10) - 2.0 * dot(diag2, l20) - vt(2, 0), li0)
        off10 = dot(y_of(1, 0) - 2.0 * dot(diag1, l10) - dot(off12, l20) - vt(1, 0), li0)
        off02, off01 = off20.T, off10.T
        diag0 = diag_adjoint(0, g_of(0) - vt(0, 0) - dot(off01, l10) - dot(off02, l20))
        whole = {
            (0, 0): diag0, (1, 1): diag1, (2, 2): diag2,
            (1, 0): 0.5 * off10, (2, 0): 0.5 * off20, (2, 1): 0.5 * off21,
            (0, 1): 0.5 * off01, (0, 2): 0.5 * off02, (1, 2): 0.5 * off12,
        }
        for i in range(STEPS):
            for j in range(STEPS):
                wp_ref[pl.ds(4 * i * B + j, B, stride=4), :] = whole[i, j]
        start = pl.multiple_of(48 * lax.axis_index("col"), 16)
        cut_ref[...] = wp_ref[pl.ds(start, 48), :]
        for k in range(STEPS):
            out_ref[:, k * B : (k + 1) * B] = cut_ref[pl.ds(k, 12, stride=4), :]


def route_kernel(mine_ref, other_ref, out_ref, sum_ref, own_ref):
    mine, other = mine_ref[...], other_ref[...]
    corner = mine[0:48] + other[0:48]
    inverse = mine[48:96] + other[48:96]
    sum_ref[...] = corner
    own_ref[...] = inverse
    out_ref[0] = corner
    for z in range(1, 8):
        out_ref[z] = inverse


def pack_y_kernel(sum_ref, own_ref, got_ref, y_ref, out_ref):
    corner = sum_ref[...] + jnp.sum(got_ref[1:], axis=0)
    inverse = jnp.where(lax.axis_index("row") < 2, own_ref[...], got_ref[0])
    for y in range(Y_SIZE):
        out_ref[y, 0:48, :] = corner
        out_ref[y, 48:96, :] = inverse
        out_ref[y, 96:112, :] = y_ref[y]


def pack_x_kernel(near_ref, out_ref):
    for x in range(X_SIZE):
        for y in range(Y_SIZE):
            out_ref[x, 48 * y : 48 * (y + 1), :] = near_ref[y, 0:48, :]
            out_ref[x, 384 + 12 * y : 384 + 12 * (y + 1), :] = near_ref[y, 96:108, :]


def solve_kernel(near_ref, w_ref, out_ref, yt_ref, lit_ref):
    for x in range(X_SIZE):
        yt_ref[96 * x : 96 * (x + 1), :] = w_ref[480 * x + 384 : 480 * (x + 1), :]
    for y in range(Y_SIZE):
        for k in range(STEPS):
            lit_ref[12 * y : 12 * (y + 1), k * B : (k + 1) * B] = near_ref[
                y, pl.ds(48 + k, 12, stride=4), :
            ]
    yt_ref[0:96, :] = 0.5 * dot(lit_ref[...], yt_ref[...])
    for y in range(Y_SIZE):
        out_ref[y, 0:12, :] = yt_ref[12 * y : 12 * (y + 1), :]
        out_ref[y, 12:16, :] = jnp.zeros((4, B), jnp.float32)


def output_kernel(x_ref, corner_ref, out_ref):
    for b in range(8):
        out_ref[:, b * B : (b + 1) * B] = x_ref[b, 0:12, :]

    @pl.when(lax.axis_index("row") == 0)
    def _():
        out_ref[:, 0:PW] = corner_ref[...]


def f32(*shape):
    return jax.ShapeDtypeStruct(shape, jnp.float32)


def vmem(*shape):
    return pltpu.VMEM(shape, jnp.float32)


def call(kernel, out_shape, *args, scratch=(), flops=0):
    many = isinstance(out_shape, (list, tuple))
    spec = pl.BlockSpec(memory_space=pltpu.VMEM)
    total = sum(a.size for a in args) * 4
    return pl.pallas_call(
        kernel,
        out_shape=out_shape,
        in_specs=[spec] * len(args),
        out_specs=[spec] * len(out_shape) if many else spec,
        scratch_shapes=list(scratch),
        compiler_params=PARAMS,
        cost_estimate=pl.CostEstimate(flops=flops, bytes_accessed=total, transcendentals=0),
    )(*args)


def spread(value, axis, groups):
    count = len(groups[0])
    copies = jnp.broadcast_to(value[None], (count,) + value.shape)
    return lax.all_to_all(copies, axis, 0, 0, axis_index_groups=groups)


def between_cores(value):
    return lax.ppermute(value, "row", [(r, r ^ 1) for r in range(16)])


def on_device(trail_adj, factor_panels, factor_adj):
    factor = factor_panels.T.reshape(96, B)
    adjoint = factor_adj.T.reshape(96, B)
    near = spread(factor, "col", Y_GROUPS).reshape(Y_SIZE * 96, B)
    panels = spread(near, "col", X_GROUPS).reshape(PW * 8, B)
    send, keep, ft, ft_corner = call(
        product_kernel, [f32(768, B), f32(768, B), f32(PW, 1024), f32(PW, PW)], panels, trail_adj,
        scratch=[vmem(PW, 512), vmem(1536, B)], flops=12 * 1024 * 512 * PW,
    )
    both = (keep + between_cores(send)).reshape(8, 96, B)
    pieces = lax.all_to_all(both, "row", 0, 0, axis_index_groups=Z_GROUPS)
    send_a, send_b = call(sum_kernel, [f32(48, B), f32(48, B)], pieces)
    devices = [(r, c) for r in range(16) for c in range(32)]
    to_a = [(r * 32 + c, place(r, c, c % 2)) for r, c in devices]
    to_b = [(r * 32 + c, place(r, c, 1 - c % 2)) for r, c in devices]
    got_a = lax.ppermute(send_a, ("row", "col"), to_a)
    got_b = lax.ppermute(send_b, ("row", "col"), to_b)
    fac, inv_tp = call(
        inverse_kernel, [f32(15 * B, B), f32(1536, B)], ft_corner, flops=12 * 60 * B**3,
    )
    payload, own_y = call(
        gram_kernel, [f32(96, B), f32(8, 16, B)], got_a, got_b, adjoint, ft, inv_tp,
        scratch=[vmem(96, B), vmem(12, 1024)], flops=12 * 12 * 1024 * PW,
    )
    out_u, sum_u, own = call(
        route_kernel, [f32(8, 48, B), f32(48, B), f32(48, B)], payload, between_cores(payload),
    )
    got = lax.all_to_all(out_u, "row", 0, 0, axis_index_groups=Z_GROUPS)
    near = call(pack_y_kernel, f32(8, 112, B), sum_u, own, got, own_y)
    near = lax.all_to_all(near, "col", 0, 0, axis_index_groups=Y_GROUPS)
    wide = call(pack_x_kernel, f32(4, 480, B), near)
    wide = lax.all_to_all(wide, "col", 0, 0, axis_index_groups=X_GROUPS).reshape(4 * 480, B)
    solved = call(
        solve_kernel, f32(8, 16, B), near, wide,
        scratch=[vmem(PW, B), vmem(96, PW)], flops=12 * 96 * B * PW,
    )
    rows_x = lax.all_to_all(solved, "col", 0, 0, axis_index_groups=Y_GROUPS)
    corner = call(
        corner_kernel, f32(12, PW), wide, fac,
        scratch=[vmem(PW, 512), vmem(PW, PW), vmem(1536, B), vmem(48, B)], flops=12 * 60 * B**3,
    )
    out = call(output_kernel, f32(12, 1024), rows_x, corner)
    return out.T


def solution(mesh):
    in_specs = (P("row", "col"), P("row", "col"), P("row", "col"))
    out_specs = P("row", "col")
    return jax.shard_map(
        on_device, mesh=mesh, in_specs=in_specs, out_specs=out_specs, check_vma=False
    )
```

```python
import functools

import jax
import jax.numpy as jnp
from jax import lax
from jax.experimental import pallas as pl
from jax.experimental.pallas import tpu as pltpu
from jax.sharding import PartitionSpec as P

B = 128
STEPS = 3
PW = STEPS * B
HI = lax.Precision.HIGHEST
X_SIZE, Y_SIZE = 4, 8
Y_GROUPS = [[x * Y_SIZE + y for y in range(Y_SIZE)] for x in range(X_SIZE)]
X_GROUPS = [[x * Y_SIZE + y for x in range(X_SIZE)] for y in range(Y_SIZE)]
Z_GROUPS = [[2 * z + core for z in range(8)] for core in range(2)]
PARAMS = pltpu.CompilerParams(vmem_limit_bytes=48 * 1024 * 1024)


def dot(a, b):
    return jnp.dot(a, b, precision=HI, preferred_element_type=jnp.float32)


def dot_bf16(a, b):
    return jnp.dot(a, b, preferred_element_type=jnp.float32)


def dot_nt(a, b):
    return lax.dot_general(
        a, b, (((1,), (1,)), ((), ())), precision=HI, preferred_element_type=jnp.float32
    )


def place(row, col, half):
    x, y = col // Y_SIZE, col % Y_SIZE
    x_to, y_to = (x + 2 * (row % 2) + half) % X_SIZE, (y + row // 2) % Y_SIZE
    return col // 2 * (X_SIZE * Y_SIZE) + x_to * Y_SIZE + y_to


def split(value):
    high = value.astype(jnp.bfloat16)
    return high, (value - high.astype(jnp.float32)).astype(jnp.bfloat16)


def product_kernel(f_ref, t_ref, send_ref, keep_ref, ft_ref, top_ref, acc_ref, cut_ref):
    row, col = lax.axis_index("row"), lax.axis_index("col")
    x, y = col // Y_SIZE, col % Y_SIZE
    panel = lax.broadcasted_iota(jnp.int32, (PW, B), 0) // B
    for b in range(8):
        part = f_ref[pl.ds(b, PW, stride=8), :]
        if b < STEPS:
            top_ref[:, b * B : (b + 1) * B] = part
            part = jnp.where((row > 0) | (panel < b), part, 0.0)
        ft_ref[:, b * B : (b + 1) * B] = part
    fh, fl = split(ft_ref[...])
    th, tl = split(t_ref[...])
    acc_ref[...] = dot_bf16(fh, tl) + dot_bf16(fl, th) + dot_bf16(fh, th)
    for b in range(4):
        cut_ref[pl.ds(b, PW, stride=4), :] = acc_ref[:, b * B : (b + 1) * B]
    for core, target in ((1 - row % 2, send_ref), (row % 2, keep_ref)):
        for z in range(8):
            for half in range(2):
                x_to, y_to = (x + 2 * core + half) % X_SIZE, (y + z) % Y_SIZE
                first = pl.multiple_of((x_to * Y_SIZE + y_to) * 48, 16)
                target[z * 96 + half * 48 : z * 96 + half * 48 + 48, :] = cut_ref[pl.ds(first, 48), :]


def sum_kernel(s_ref, a_ref, b_ref):
    odd = lax.axis_index("col") % 2 == 1
    low = jnp.sum(s_ref[:, 0:48, :], axis=0)
    high = jnp.sum(s_ref[:, 48:96, :], axis=0)
    a_ref[...] = jnp.where(odd, high, low)
    b_ref[...] = jnp.where(odd, low, high)


def corner_block(kind, i, j):
    lower = {(0, 0): 0, (1, 0): 1, (1, 1): 2, (2, 0): 3, (2, 1): 4, (2, 2): 5}
    if kind == "l":
        place = lower[i, j]
    elif kind == "lit":
        place = 6 + lower[j, i]
    else:
        place = 12 + i
    return slice(place * B, (place + 1) * B)


def inverse_kernel(top_ref, fac_ref, litp_ref):
    @pl.when(lax.axis_index("row") == 0)
    def _():
        rows = lax.broadcasted_iota(jnp.int32, (B, B), 0)
        cols = lax.broadcasted_iota(jnp.int32, (B, B), 1)
        lt = {}
        for j in range(STEPS):
            for i in range(j + 1):
                value = top_ref[i * B : (i + 1) * B, j * B : (j + 1) * B]
                lt[i, j] = jnp.where(rows <= cols, value, 0.0) if i == j else value
                fac_ref[corner_block("l", j, i)] = lt[i, j].T
        inv = {}
        for i in range(STEPS):
            inv[i, i] = jnp.where(rows == cols, 1.0 / lt[i, i], 0.0)
        size = 1
        while size < B:
            mask = (rows // (2 * size) == cols // (2 * size)) & (rows // size < cols // size)
            step = [dot(inv[i, i], jnp.where(mask, lt[i, i], 0.0)) for i in range(STEPS)]
            for i in range(STEPS):
                inv[i, i] = inv[i, i] - dot(step[i], inv[i, i])
            size *= 2
        inv[0, 1] = -dot(dot(inv[0, 0], lt[0, 1]), inv[1, 1])
        inv[1, 2] = -dot(dot(inv[1, 1], lt[1, 2]), inv[2, 2])
        inv[0, 2] = -dot(dot(inv[0, 0], lt[0, 2]) + dot(inv[0, 1], lt[1, 2]), inv[2, 2])
        zero = jnp.zeros((B, B), jnp.float32)
        for i in range(STEPS):
            for j in range(4):
                litp_ref[pl.ds(4 * i * B + j, B, stride=4), :] = inv.get((i, j), zero)
            for j in range(i, STEPS):
                fac_ref[corner_block("lit", i, j)] = inv[i, j]
            fac_ref[corner_block("li", i, i)] = inv[i, i].T


def gram_kernel(ra_ref, rb_ref, g_ref, ft_ref, litp_ref, pay_ref, y_ref, half_ref, ym_ref):
    row, col = lax.axis_index("row"), lax.axis_index("col")
    first = (col // Y_SIZE + row // 4) % 2 == 0
    ra, rb = ra_ref[...], rb_ref[...]
    half_ref[0:48, :] = jnp.where(first, ra, rb)
    half_ref[48:96, :] = jnp.where(first, rb, ra)
    panel = (12 * col + lax.broadcasted_iota(jnp.int32, (12, B), 0)) // B
    top, diag = [], jnp.zeros((12, B), jnp.float32)
    for b in range(8):
        g = g_ref[:, b * B : (b + 1) * B]
        y = g - 2.0 * half_ref[pl.ds(b // 4 * 48 + b % 4, 12, stride=4), :]
        y_ref[b, 0:12, :] = y
        y_ref[b, 12:16, :] = jnp.zeros((4, B), jnp.float32)
        if b < STEPS:
            top.append(y)
            diag = jnp.where(panel == b, g, diag)
            y = jnp.where(row > 0, y, 0.0)
        ym_ref[:, b * B : (b + 1) * B] = y
    gram = dot_nt(ym_ref[...], ft_ref[...])
    for k in range(STEPS):
        below = jnp.where(row == 0, top[k], 0.0)
        pay_ref[pl.ds(24 * (k // 2) + k % 2, 12, stride=2), :] = jnp.where(
            panel >= k, gram[:, k * B : (k + 1) * B], below
        )
    pay_ref[pl.ds(25, 12, stride=2), :] = jnp.where(row == 0, diag, 0.0)
    own = litp_ref[pl.ds(pl.multiple_of(48 * col, 16), 48), :]
    pay_ref[48:96, :] = jnp.where(row == 0, own, 0.0)


def corner_kernel(w_ref, other_ref, fac_ref, out_ref, u_ref, vt_ref, wp_ref, cut_ref):
    @pl.when(lax.axis_index("row") == 0)
    def _():
        for x in range(X_SIZE):
            for k in range(4):
                half_ref = w_ref if k < 2 else other_ref
                u_ref[96 * x : 96 * (x + 1), k * B : (k + 1) * B] = half_ref[
                    pl.ds(288 * x + k % 2, 96, stride=2), :
                ]
        rows = lax.broadcasted_iota(jnp.int32, (B, B), 0)
        cols = lax.broadcasted_iota(jnp.int32, (B, B), 1)

        def blk(i, j):
            return (slice(i * B, (i + 1) * B), slice(j * B, (j + 1) * B))

        def fac(kind, i, j):
            return fac_ref[corner_block(kind, i, j)]

        for j in range(STEPS):
            for k in range(j + 1):
                terms = [dot(fac("lit", j, i), u_ref[blk(i, k)]) for i in range(j, STEPS)]
                vt_ref[blk(j, k)] = functools.reduce(jnp.add, terms)

        def vt(j, k):
            return vt_ref[blk(j, k)]

        def y_of(j, k):
            return u_ref[blk(k, j)].T

        def g_of(k):
            return u_ref[blk(k, STEPS)]

        def diag_adjoint(k, total_t):
            product_t = dot(total_t, fac("l", k, k))
            halved_t = jnp.where(rows < cols, product_t, jnp.where(rows == cols, 0.5 * product_t, 0.0))
            sandwich = dot(dot(fac("lit", k, k), halved_t), fac("li", k, k))
            return 0.5 * (sandwich + sandwich.T)

        l10, l20, l21 = fac("l", 1, 0), fac("l", 2, 0), fac("l", 2, 1)
        li0, li1 = fac("li", 0, 0), fac("li", 1, 1)
        diag2 = diag_adjoint(2, g_of(2) - vt(2, 2))
        off21 = dot(y_of(2, 1) - 2.0 * dot(diag2, l21) - vt(2, 1), li1)
        off12 = off21.T
        diag1 = diag_adjoint(1, g_of(1) - vt(1, 1) - dot(off12, l21))
        off20 = dot(y_of(2, 0) - dot(off21, l10) - 2.0 * dot(diag2, l20) - vt(2, 0), li0)
        off10 = dot(y_of(1, 0) - 2.0 * dot(diag1, l10) - dot(off12, l20) - vt(1, 0), li0)
        off02, off01 = off20.T, off10.T
        diag0 = diag_adjoint(0, g_of(0) - vt(0, 0) - dot(off01, l10) - dot(off02, l20))
        whole = {
            (0, 0): diag0, (1, 1): diag1, (2, 2): diag2,
            (1, 0): 0.5 * off10, (2, 0): 0.5 * off20, (2, 1): 0.5 * off21,
            (0, 1): 0.5 * off01, (0, 2): 0.5 * off02, (1, 2): 0.5 * off12,
        }
        for i in range(STEPS):
            for j in range(STEPS):
                wp_ref[pl.ds(4 * i * B + j, B, stride=4), :] = whole[i, j]
        start = pl.multiple_of(48 * lax.axis_index("col"), 16)
        cut_ref[...] = wp_ref[pl.ds(start, 48), :]
        for k in range(STEPS):
            out_ref[:, k * B : (k + 1) * B] = cut_ref[pl.ds(k, 12, stride=4), :]


def route_kernel(mine_ref, other_ref, out_ref, sum_ref, own_ref):
    mine, other = mine_ref[...], other_ref[...]
    corner = mine[0:48] + other[0:48]
    inverse = mine[48:96] + other[48:96]
    sum_ref[...] = corner
    own_ref[...] = inverse
    out_ref[0] = corner
    for z in range(1, 8):
        out_ref[z] = inverse


def pack_y_kernel(sum_ref, own_ref, got_ref, y_ref, out_ref):
    row = lax.axis_index("row")
    corner = sum_ref[...] + jnp.sum(got_ref[1:], axis=0)
    corner = jnp.where(row % 2 == 0, corner[0:24], corner[24:48])
    inverse = jnp.where(row < 2, own_ref[...], got_ref[0])
    for y in range(Y_SIZE):
        out_ref[y, 0:24, :] = corner
        out_ref[y, 24:72, :] = inverse
        out_ref[y, 72:88, :] = y_ref[y]


def pack_x_kernel(near_ref, out_ref):
    for x in range(X_SIZE):
        for y in range(Y_SIZE):
            out_ref[x, 24 * y : 24 * (y + 1), :] = near_ref[y, 0:24, :]
            out_ref[x, 192 + 12 * y : 192 + 12 * (y + 1), :] = near_ref[y, 72:84, :]


def solve_kernel(near_ref, w_ref, out_ref, yt_ref, lit_ref):
    for x in range(X_SIZE):
        yt_ref[96 * x : 96 * (x + 1), :] = w_ref[288 * x + 192 : 288 * (x + 1), :]
    for y in range(Y_SIZE):
        for k in range(STEPS):
            lit_ref[12 * y : 12 * (y + 1), k * B : (k + 1) * B] = near_ref[
                y, pl.ds(24 + k, 12, stride=4), :
            ]
    yt_ref[0:96, :] = 0.5 * dot(lit_ref[...], yt_ref[...])
    for y in range(Y_SIZE):
        out_ref[y, 0:12, :] = yt_ref[12 * y : 12 * (y + 1), :]
        out_ref[y, 12:16, :] = jnp.zeros((4, B), jnp.float32)


def output_kernel(x_ref, corner_ref, out_ref):
    for b in range(8):
        out_ref[:, b * B : (b + 1) * B] = x_ref[b, 0:12, :]

    @pl.when(lax.axis_index("row") == 0)
    def _():
        out_ref[:, 0:PW] = corner_ref[...]


def f32(*shape):
    return jax.ShapeDtypeStruct(shape, jnp.float32)


def vmem(*shape):
    return pltpu.VMEM(shape, jnp.float32)


def call(kernel, out_shape, *args, scratch=(), flops=0):
    many = isinstance(out_shape, (list, tuple))
    spec = pl.BlockSpec(memory_space=pltpu.VMEM)
    total = sum(a.size for a in args) * 4
    return pl.pallas_call(
        kernel,
        out_shape=out_shape,
        in_specs=[spec] * len(args),
        out_specs=[spec] * len(out_shape) if many else spec,
        scratch_shapes=list(scratch),
        compiler_params=PARAMS,
        cost_estimate=pl.CostEstimate(flops=flops, bytes_accessed=total, transcendentals=0),
    )(*args)


def spread(value, axis, groups):
    count = len(groups[0])
    copies = jnp.broadcast_to(value[None], (count,) + value.shape)
    return lax.all_to_all(copies, axis, 0, 0, axis_index_groups=groups)


def between_cores(value):
    return lax.ppermute(value, "row", [(r, r ^ 1) for r in range(16)])


def on_device(trail_adj, factor_panels, factor_adj):
    factor = factor_panels.T.reshape(96, B)
    near = spread(factor, "col", Y_GROUPS).reshape(Y_SIZE * 96, B)
    panels = spread(near, "col", X_GROUPS).reshape(PW * 8, B)
    send, keep, ft, ft_corner = call(
        product_kernel, [f32(768, B), f32(768, B), f32(PW, 1024), f32(PW, PW)], panels, trail_adj,
        scratch=[vmem(PW, 512), vmem(1536, B)], flops=12 * 1024 * 512 * PW,
    )
    both = (keep + between_cores(send)).reshape(8, 96, B)
    pieces = lax.all_to_all(both, "row", 0, 0, axis_index_groups=Z_GROUPS)
    send_a, send_b = call(sum_kernel, [f32(48, B), f32(48, B)], pieces)
    devices = [(r, c) for r in range(16) for c in range(32)]
    to_a = [(r * 32 + c, place(r, c, c % 2)) for r, c in devices]
    to_b = [(r * 32 + c, place(r, c, 1 - c % 2)) for r, c in devices]
    got_a = lax.ppermute(send_a, ("row", "col"), to_a)
    got_b = lax.ppermute(send_b, ("row", "col"), to_b)
    fac, inv_tp = call(
        inverse_kernel, [f32(15 * B, B), f32(1536, B)], ft_corner, flops=12 * 60 * B**3,
    )
    payload, own_y = call(
        gram_kernel, [f32(96, B), f32(8, 16, B)], got_a, got_b, factor_adj.T, ft, inv_tp,
        scratch=[vmem(96, B), vmem(12, 1024)], flops=12 * 12 * 1024 * PW,
    )
    out_u, sum_u, own = call(
        route_kernel, [f32(8, 48, B), f32(48, B), f32(48, B)], payload, between_cores(payload),
    )
    got = lax.all_to_all(out_u, "row", 0, 0, axis_index_groups=Z_GROUPS)
    near = call(pack_y_kernel, f32(8, 88, B), sum_u, own, got, own_y)
    near = lax.all_to_all(near, "col", 0, 0, axis_index_groups=Y_GROUPS)
    wide = call(pack_x_kernel, f32(4, 288, B), near)
    wide = lax.all_to_all(wide, "col", 0, 0, axis_index_groups=X_GROUPS).reshape(4 * 288, B)
    other = between_cores(wide)
    solved = call(
        solve_kernel, f32(8, 16, B), near, wide,
        scratch=[vmem(PW, B), vmem(96, PW)], flops=12 * 96 * B * PW,
    )
    rows_x = lax.all_to_all(solved, "col", 0, 0, axis_index_groups=Y_GROUPS)
    corner = call(
        corner_kernel, f32(12, PW), wide, other, fac,
        scratch=[vmem(PW, 512), vmem(PW, PW), vmem(1536, B), vmem(48, B)], flops=12 * 60 * B**3,
    )
    out = call(output_kernel, f32(12, 1024), rows_x, corner)
    return out.T


def solution(mesh):
    in_specs = (P("row", "col"), P("row", "col"), P("row", "col"))
    out_specs = P("row", "col")
    return jax.shard_map(
        on_device, mesh=mesh, in_specs=in_specs, out_specs=out_specs, check_vma=False
    )
```

```python
import functools

import jax
import jax.numpy as jnp
from jax import lax
from jax.experimental import pallas as pl
from jax.experimental.pallas import tpu as pltpu
from jax.sharding import PartitionSpec as P

B = 128
STEPS = 3
PW = STEPS * B
HI = lax.Precision.HIGHEST
X_SIZE, Y_SIZE = 4, 8
Y_GROUPS = [[x * Y_SIZE + y for y in range(Y_SIZE)] for x in range(X_SIZE)]
X_GROUPS = [[x * Y_SIZE + y for x in range(X_SIZE)] for y in range(Y_SIZE)]
Z_GROUPS = [[2 * z + core for z in range(8)] for core in range(2)]
PARAMS = pltpu.CompilerParams(vmem_limit_bytes=48 * 1024 * 1024)


def dot(a, b):
    return jnp.dot(a, b, precision=HI, preferred_element_type=jnp.float32)


def dot_bf16(a, b):
    return jnp.dot(a, b, preferred_element_type=jnp.float32)


def dot_nt(a, b):
    return lax.dot_general(a, b, (((1,), (1,)), ((), ())), preferred_element_type=jnp.float32)


def place(row, col, half):
    x, y = col // Y_SIZE, col % Y_SIZE
    x_to, y_to = (x + 2 * (row % 2) + half) % X_SIZE, (y + row // 2) % Y_SIZE
    return col // 2 * (X_SIZE * Y_SIZE) + x_to * Y_SIZE + y_to


def split(value):
    high = value.astype(jnp.bfloat16)
    return high, (value - high.astype(jnp.float32)).astype(jnp.bfloat16)


def add_kernel(a_ref, b_ref, _, out_ref):
    out_ref[...] = a_ref[...] + b_ref[...]


def product_kernel(f_ref, t_ref, send_ref, keep_ref, fh_ref, fl_ref, top_ref, acc_ref, cut_ref):
    row, col = lax.axis_index("row"), lax.axis_index("col")
    x, y = col // Y_SIZE, col % Y_SIZE
    panel = lax.broadcasted_iota(jnp.int32, (PW, B), 0) // B
    for b in range(8):
        part = f_ref[pl.ds(b, PW, stride=8), :]
        if b < STEPS:
            top_ref[:, b * B : (b + 1) * B] = part
            part = jnp.where((row > 0) | (panel < b), part, 0.0)
        fh_ref[:, b * B : (b + 1) * B], fl_ref[:, b * B : (b + 1) * B] = split(part)
    fh, fl = fh_ref[...], fl_ref[...]
    th, tl = split(t_ref[...])
    acc_ref[...] = dot_bf16(fh, tl) + dot_bf16(fl, th) + dot_bf16(fh, th)
    for b in range(4):
        cut_ref[pl.ds(b, PW, stride=4), :] = acc_ref[:, b * B : (b + 1) * B]
    for core, target in ((1 - row % 2, send_ref), (row % 2, keep_ref)):
        for z in range(8):
            for half in range(2):
                x_to, y_to = (x + 2 * core + half) % X_SIZE, (y + z) % Y_SIZE
                first = pl.multiple_of((x_to * Y_SIZE + y_to) * 48, 16)
                target[z * 96 + half * 48 : z * 96 + half * 48 + 48, :] = cut_ref[pl.ds(first, 48), :]


def sum_kernel(s_ref, a_ref, b_ref):
    odd = lax.axis_index("col") % 2 == 1
    low = jnp.sum(s_ref[:, 0:48, :], axis=0)
    high = jnp.sum(s_ref[:, 48:96, :], axis=0)
    a_ref[...] = jnp.where(odd, high, low)
    b_ref[...] = jnp.where(odd, low, high)


def corner_block(kind, i, j):
    lower = {(0, 0): 0, (1, 0): 1, (1, 1): 2, (2, 0): 3, (2, 1): 4, (2, 2): 5}
    if kind == "l":
        place = lower[i, j]
    elif kind == "lit":
        place = 6 + lower[j, i]
    else:
        place = 12 + i
    return slice(place * B, (place + 1) * B)


def inverse_kernel(top_ref, fac_ref, litp_ref):
    @pl.when(lax.axis_index("row") == 0)
    def _():
        rows = lax.broadcasted_iota(jnp.int32, (B, B), 0)
        cols = lax.broadcasted_iota(jnp.int32, (B, B), 1)
        lt = {}
        for j in range(STEPS):
            for i in range(j + 1):
                value = top_ref[i * B : (i + 1) * B, j * B : (j + 1) * B]
                lt[i, j] = jnp.where(rows <= cols, value, 0.0) if i == j else value
                fac_ref[corner_block("l", j, i)] = lt[i, j].T
        inv = {}
        for i in range(STEPS):
            inv[i, i] = jnp.where(rows == cols, 1.0 / lt[i, i], 0.0)
        size = 1
        while size < B:
            mask = (rows // (2 * size) == cols // (2 * size)) & (rows // size < cols // size)
            step = [dot(inv[i, i], jnp.where(mask, lt[i, i], 0.0)) for i in range(STEPS)]
            for i in range(STEPS):
                inv[i, i] = inv[i, i] - dot(step[i], inv[i, i])
            size *= 2
        inv[0, 1] = -dot(dot(inv[0, 0], lt[0, 1]), inv[1, 1])
        inv[1, 2] = -dot(dot(inv[1, 1], lt[1, 2]), inv[2, 2])
        inv[0, 2] = -dot(dot(inv[0, 0], lt[0, 2]) + dot(inv[0, 1], lt[1, 2]), inv[2, 2])
        zero = jnp.zeros((B, B), jnp.float32)
        for i in range(STEPS):
            for j in range(4):
                litp_ref[pl.ds(4 * i * B + j, B, stride=4), :] = inv.get((i, j), zero)
            for j in range(i, STEPS):
                fac_ref[corner_block("lit", i, j)] = inv[i, j]
            fac_ref[corner_block("li", i, i)] = inv[i, i].T


def gram_kernel(ra_ref, rb_ref, g_ref, fh_ref, fl_ref, litp_ref, pay_ref, y_ref, half_ref, ym_ref, own_ref):
    row, col = lax.axis_index("row"), lax.axis_index("col")
    first = (col // Y_SIZE + row // 4) % 2 == 0
    ra, rb = ra_ref[...], rb_ref[...]
    half_ref[0:48, :] = jnp.where(first, ra, rb)
    half_ref[48:96, :] = jnp.where(first, rb, ra)
    panel = (12 * col + lax.broadcasted_iota(jnp.int32, (12, B), 0)) // B
    top, diag = [], jnp.zeros((12, B), jnp.float32)
    for b in range(8):
        g = g_ref[:, b * B : (b + 1) * B]
        y = g - 2.0 * half_ref[pl.ds(b // 4 * 48 + b % 4, 12, stride=4), :]
        y_ref[b, 0:12, :] = y
        y_ref[b, 12:16, :] = jnp.zeros((4, B), jnp.float32)
        if b < STEPS:
            top.append(y)
            diag = jnp.where(panel == b, g, diag)
            y = jnp.where(row > 0, y, 0.0)
        ym_ref[:, b * B : (b + 1) * B] = y
    yh, yl = split(ym_ref[...])
    fh = fh_ref[...]
    gram = dot_nt(yh, fl_ref[...]) + dot_nt(yl, fh) + dot_nt(yh, fh)
    for k in range(STEPS):
        below = jnp.where(row == 0, top[k], 0.0)
        part = jnp.where(panel >= k, gram[:, k * B : (k + 1) * B], below)
        if k < 2:
            pay_ref[pl.ds(k, 12, stride=2), :] = part
        else:
            pay_ref[24:36, :] = part
    pay_ref[36:48, :] = jnp.where(row == 0, diag, 0.0)
    own_ref[...] = jnp.where(row == 0, litp_ref[pl.ds(pl.multiple_of(48 * col, 16), 48), :], 0.0)
    for k in range(STEPS):
        pay_ref[pl.ds(48 + k, 12, stride=3), :] = own_ref[pl.ds(k, 12, stride=4), :]
    pay_ref[84:88, :] = jnp.zeros((4, B), jnp.float32)


def corner_kernel(mine_ref, other_ref, fac_ref, out_ref, u_ref, vt_ref, wp_ref, cut_ref):
    @pl.when(lax.axis_index("row") == 0)
    def _():
        for x in range(X_SIZE):
            for k in range(4):
                half_ref = mine_ref if k < 2 else other_ref
                u_ref[96 * x : 96 * (x + 1), k * B : (k + 1) * B] = half_ref[
                    pl.ds(192 * x + k % 2, 96, stride=2), :
                ]
        rows = lax.broadcasted_iota(jnp.int32, (B, B), 0)
        cols = lax.broadcasted_iota(jnp.int32, (B, B), 1)

        def blk(i, j):
            return (slice(i * B, (i + 1) * B), slice(j * B, (j + 1) * B))

        def fac(kind, i, j):
            return fac_ref[corner_block(kind, i, j)]

        for j in range(STEPS):
            for k in range(j + 1):
                terms = [dot(fac("lit", j, i), u_ref[blk(i, k)]) for i in range(j, STEPS)]
                vt_ref[blk(j, k)] = functools.reduce(jnp.add, terms)

        def vt(j, k):
            return vt_ref[blk(j, k)]

        def y_of(j, k):
            return u_ref[blk(k, j)].T

        def g_of(k):
            return u_ref[blk(k, STEPS)]

        def diag_adjoint(k, total_t):
            product_t = dot(total_t, fac("l", k, k))
            halved_t = jnp.where(rows < cols, product_t, jnp.where(rows == cols, 0.5 * product_t, 0.0))
            sandwich = dot(dot(fac("lit", k, k), halved_t), fac("li", k, k))
            return 0.5 * (sandwich + sandwich.T)

        l10, l20, l21 = fac("l", 1, 0), fac("l", 2, 0), fac("l", 2, 1)
        li0, li1 = fac("li", 0, 0), fac("li", 1, 1)
        diag2 = diag_adjoint(2, g_of(2) - vt(2, 2))
        off21 = dot(y_of(2, 1) - 2.0 * dot(diag2, l21) - vt(2, 1), li1)
        off12 = off21.T
        diag1 = diag_adjoint(1, g_of(1) - vt(1, 1) - dot(off12, l21))
        off20 = dot(y_of(2, 0) - dot(off21, l10) - 2.0 * dot(diag2, l20) - vt(2, 0), li0)
        off10 = dot(y_of(1, 0) - 2.0 * dot(diag1, l10) - dot(off12, l20) - vt(1, 0), li0)
        off02, off01 = off20.T, off10.T
        diag0 = diag_adjoint(0, g_of(0) - vt(0, 0) - dot(off01, l10) - dot(off02, l20))
        whole = {
            (0, 0): diag0, (1, 1): diag1, (2, 2): diag2,
            (1, 0): 0.5 * off10, (2, 0): 0.5 * off20, (2, 1): 0.5 * off21,
            (0, 1): 0.5 * off01, (0, 2): 0.5 * off02, (1, 2): 0.5 * off12,
        }
        for i in range(STEPS):
            for j in range(STEPS):
                wp_ref[pl.ds(4 * i * B + j, B, stride=4), :] = whole[i, j]
        start = pl.multiple_of(48 * lax.axis_index("col"), 16)
        cut_ref[...] = wp_ref[pl.ds(start, 48), :]
        for k in range(STEPS):
            out_ref[:, k * B : (k + 1) * B] = cut_ref[pl.ds(k, 12, stride=4), :]


def route_kernel(mine_ref, other_ref, out_ref, sum_ref):
    total = mine_ref[...] + other_ref[...]
    sum_ref[...] = total
    out_ref[0] = total[0:40]
    for z in range(1, 8):
        out_ref[z] = total[48:88]


def pack_y_kernel(sum_ref, got_ref, y_ref, out_ref):
    row = lax.axis_index("row")
    corner = sum_ref[0:36, :] + jnp.sum(got_ref[1:, 0:36, :], axis=0)
    inverse = jnp.where(row < 2, sum_ref[48:84, :], got_ref[0, 0:36, :])
    first, second = corner[24:36], sum_ref[36:48, :]
    for y in range(Y_SIZE):
        out_ref[y, pl.ds(0, 12, stride=2), :] = first
        out_ref[y, pl.ds(1, 12, stride=2), :] = second
        out_ref[y, 24:60, :] = inverse
        out_ref[y, 60:72, :] = y_ref[y, 0:12, :]

    @pl.when(row % 2 == 0)
    def _():
        for y in range(Y_SIZE):
            out_ref[y, 0:24, :] = corner[0:24]


def pack_x_kernel(near_ref, out_ref):
    for x in range(X_SIZE):
        for y in range(Y_SIZE):
            out_ref[x, 24 * y : 24 * (y + 1), :] = near_ref[y, 0:24, :]
            out_ref[x, 192 + 12 * y : 192 + 12 * (y + 1), :] = near_ref[y, 60:72, :]


def solve_kernel(near_ref, w_ref, out_ref, half_ref, yt_ref, lit_ref):
    for x in range(X_SIZE):
        yt_ref[96 * x : 96 * (x + 1), :] = w_ref[288 * x + 192 : 288 * (x + 1), :]
    for y in range(Y_SIZE):
        for k in range(STEPS):
            lit_ref[12 * y : 12 * (y + 1), k * B : (k + 1) * B] = near_ref[
                y, pl.ds(24 + k, 12, stride=3), :
            ]
    yt_ref[0:96, :] = 0.5 * dot(lit_ref[...], yt_ref[...])
    for y in range(Y_SIZE):
        out_ref[y, 0:12, :] = yt_ref[12 * y : 12 * (y + 1), :]
        out_ref[y, 12:16, :] = jnp.zeros((4, B), jnp.float32)
    for x in range(X_SIZE):
        half_ref[192 * x : 192 * (x + 1), :] = w_ref[288 * x : 288 * x + 192, :]


def output_kernel(x_ref, corner_ref, out_ref):
    for b in range(8):
        out_ref[:, b * B : (b + 1) * B] = x_ref[b, 0:12, :]

    @pl.when(lax.axis_index("row") == 0)
    def _():
        out_ref[:, 0:PW] = corner_ref[...]


def f32(*shape):
    return jax.ShapeDtypeStruct(shape, jnp.float32)


def bf16(*shape):
    return jax.ShapeDtypeStruct(shape, jnp.bfloat16)


def vmem(*shape):
    return pltpu.VMEM(shape, jnp.float32)


def call(kernel, out_shape, *args, scratch=(), flops=0, after=()):
    many = isinstance(out_shape, (list, tuple))
    spec = pl.BlockSpec(memory_space=pltpu.VMEM)
    total = sum(a.size for a in args) * 4
    return pl.pallas_call(
        kernel,
        out_shape=out_shape,
        in_specs=[spec] * len(args) + [pl.BlockSpec(memory_space=pl.ANY)] * len(after),
        out_specs=[spec] * len(out_shape) if many else spec,
        scratch_shapes=list(scratch),
        compiler_params=PARAMS,
        cost_estimate=pl.CostEstimate(flops=flops, bytes_accessed=total, transcendentals=0),
    )(*args, *after)


def spread(value, axis, groups):
    count = len(groups[0])
    copies = jnp.broadcast_to(value[None], (count,) + value.shape)
    return lax.all_to_all(copies, axis, 0, 0, axis_index_groups=groups)


def between_cores(value):
    return lax.ppermute(value, "row", [(r, r ^ 1) for r in range(16)])


def on_device(trail_adj, factor_panels, factor_adj):
    factor = factor_panels.T.reshape(96, B)
    near = spread(factor, "col", Y_GROUPS).reshape(Y_SIZE * 96, B)
    panels = spread(near, "col", X_GROUPS).reshape(PW * 8, B)
    send, keep, panel_high, panel_low, ft_corner = call(
        product_kernel, [f32(768, B), f32(768, B), bf16(PW, 1024), bf16(PW, 1024), f32(PW, PW)], panels, trail_adj,
        scratch=[vmem(PW, 512), vmem(1536, B)], flops=12 * 1024 * 512 * PW,
    )
    fac, inv_tp = call(
        inverse_kernel, [f32(15 * B, B), f32(1536, B)], ft_corner, flops=12 * 60 * B**3,
    )
    both = call(add_kernel, f32(768, B), keep, between_cores(send), after=[inv_tp]).reshape(8, 96, B)
    pieces = lax.all_to_all(both, "row", 0, 0, axis_index_groups=Z_GROUPS)
    send_a, send_b = call(sum_kernel, [f32(48, B), f32(48, B)], pieces)
    devices = [(r, c) for r in range(16) for c in range(32)]
    to_a = [(r * 32 + c, place(r, c, c % 2)) for r, c in devices]
    to_b = [(r * 32 + c, place(r, c, 1 - c % 2)) for r, c in devices]
    got_a = lax.ppermute(send_a, ("row", "col"), to_a)
    got_b = lax.ppermute(send_b, ("row", "col"), to_b)
    payload, own_y = call(
        gram_kernel, [f32(88, B), f32(8, 16, B)], got_a, got_b, factor_adj.T, panel_high, panel_low, inv_tp,
        scratch=[vmem(96, B), vmem(12, 1024), vmem(48, B)], flops=12 * 12 * 1024 * PW,
    )
    out_u, sum_u = call(
        route_kernel, [f32(8, 40, B), f32(88, B)], payload, between_cores(payload),
    )
    got = lax.all_to_all(out_u, "row", 0, 0, axis_index_groups=Z_GROUPS)
    near = call(pack_y_kernel, f32(8, 72, B), sum_u, got, own_y)
    near = lax.all_to_all(near, "col", 0, 0, axis_index_groups=Y_GROUPS)
    wide = call(pack_x_kernel, f32(4, 288, B), near)
    wide = lax.all_to_all(wide, "col", 0, 0, axis_index_groups=X_GROUPS).reshape(4 * 288, B)
    solved, half = call(
        solve_kernel, [f32(8, 16, B), f32(768, B)], near, wide,
        scratch=[vmem(PW, B), vmem(96, PW)], flops=12 * 96 * B * PW,
    )
    rows_x = lax.all_to_all(solved, "col", 0, 0, axis_index_groups=Y_GROUPS)
    corner = call(
        corner_kernel, f32(12, PW), half, between_cores(half), fac,
        scratch=[vmem(PW, 512), vmem(PW, PW), vmem(1536, B), vmem(48, B)],
    )
    out = call(output_kernel, f32(12, 1024), rows_x, corner)
    return out.T


def solution(mesh):
    in_specs = (P("row", "col"), P("row", "col"), P("row", "col"))
    out_specs = P("row", "col")
    return jax.shard_map(
        on_device, mesh=mesh, in_specs=in_specs, out_specs=out_specs, check_vma=False
    )
```

```python
import functools

import jax
import jax.numpy as jnp
from jax import lax
from jax.experimental import pallas as pl
from jax.experimental.pallas import tpu as pltpu
from jax.sharding import PartitionSpec as P

B = 128
STEPS = 3
PW = STEPS * B
HI = lax.Precision.HIGHEST
X_SIZE, Y_SIZE = 4, 8
Y_GROUPS = [[x * Y_SIZE + y for y in range(Y_SIZE)] for x in range(X_SIZE)]
X_GROUPS = [[x * Y_SIZE + y for x in range(X_SIZE)] for y in range(Y_SIZE)]
Z_GROUPS = [[2 * z + core for z in range(8)] for core in range(2)]
PARAMS = pltpu.CompilerParams(vmem_limit_bytes=48 * 1024 * 1024)


def dot(a, b):
    return jnp.dot(a, b, precision=HI, preferred_element_type=jnp.float32)


def dot_bf16(a, b):
    return jnp.dot(a, b, preferred_element_type=jnp.float32)


def dot_nt(a, b):
    return lax.dot_general(a, b, (((1,), (1,)), ((), ())), preferred_element_type=jnp.float32)


def place(row, col, half):
    x, y = col // Y_SIZE, col % Y_SIZE
    x_to, y_to = (x + 2 * (row % 2) + half) % X_SIZE, (y + row // 2 + 12 - col // 4) % Y_SIZE
    return col // 2 * (X_SIZE * Y_SIZE) + x_to * Y_SIZE + y_to


def split(value):
    high = value.astype(jnp.bfloat16)
    return high, (value - high.astype(jnp.float32)).astype(jnp.bfloat16)


def add_kernel(a_ref, b_ref, _, out_ref):
    out_ref[...] = a_ref[...] + b_ref[...]


def product_kernel(
    f_ref, t_hbm_ref, send_ref, keep_ref, fh_ref, fl_ref, top_ref, acc_ref, cut_ref, t_ref, sems
):
    parts = [pl.ds(256 * q, 256) for q in range(4)]
    copies = [
        pltpu.make_async_copy(t_hbm_ref.at[part], t_ref.at[part], sems.at[q])
        for q, part in enumerate(parts)
    ]
    for copy in copies:
        copy.start()
    row, col = lax.axis_index("row"), lax.axis_index("col")
    x, y = col // Y_SIZE, col % Y_SIZE
    panel = lax.broadcasted_iota(jnp.int32, (PW, B), 0) // B
    for b in range(8):
        part = f_ref[pl.ds(b, PW, stride=8), :]
        if b < STEPS:
            top_ref[:, b * B : (b + 1) * B] = part
            part = jnp.where((row > 0) | (panel < b), part, 0.0)
        fh_ref[:, b * B : (b + 1) * B], fl_ref[:, b * B : (b + 1) * B] = split(part)
    for q, part in enumerate(parts):
        copies[q].wait()
        fh, fl = fh_ref[:, part], fl_ref[:, part]
        th, tl = split(t_ref[part, :])
        term = dot_bf16(fh, tl) + dot_bf16(fl, th) + dot_bf16(fh, th)
        acc_ref[...] = term if q == 0 else acc_ref[...] + term
    for b in range(4):
        cut_ref[pl.ds(b, PW, stride=4), :] = acc_ref[:, b * B : (b + 1) * B]
    for core, target in ((1 - row % 2, send_ref), (row % 2, keep_ref)):
        for z in range(8):
            for half in range(2):
                x_to, y_to = (x + 2 * core + half) % X_SIZE, (y + z + 12 - col // 4) % Y_SIZE
                first = pl.multiple_of((x_to * Y_SIZE + y_to) * 48, 16)
                target[z * 96 + half * 48 : z * 96 + half * 48 + 48, :] = cut_ref[pl.ds(first, 48), :]


def sum_kernel(s_ref, a_ref, b_ref):
    odd = lax.axis_index("col") % 2 == 1
    low = jnp.sum(s_ref[:, 0:48, :], axis=0)
    high = jnp.sum(s_ref[:, 48:96, :], axis=0)
    a_ref[...] = jnp.where(odd, high, low)
    b_ref[...] = jnp.where(odd, low, high)


def corner_block(kind, i, j):
    lower = {(0, 0): 0, (1, 0): 1, (1, 1): 2, (2, 0): 3, (2, 1): 4, (2, 2): 5}
    if kind == "l":
        place = lower[i, j]
    elif kind == "lit":
        place = 6 + lower[j, i]
    else:
        place = 12 + i
    return slice(place * B, (place + 1) * B)


def inverse_kernel(top_ref, fac_ref, litp_ref):
    @pl.when(lax.axis_index("row") == 0)
    def _():
        rows = lax.broadcasted_iota(jnp.int32, (B, B), 0)
        cols = lax.broadcasted_iota(jnp.int32, (B, B), 1)
        lt = {}
        for j in range(STEPS):
            for i in range(j + 1):
                value = top_ref[i * B : (i + 1) * B, j * B : (j + 1) * B]
                lt[i, j] = jnp.where(rows <= cols, value, 0.0) if i == j else value
                fac_ref[corner_block("l", j, i)] = lt[i, j].T
        inv = {}
        for i in range(STEPS):
            inv[i, i] = jnp.where(rows == cols, 1.0 / lt[i, i], 0.0)
        size = 1
        while size < B:
            mask = (rows // (2 * size) == cols // (2 * size)) & (rows // size < cols // size)
            step = [dot(inv[i, i], jnp.where(mask, lt[i, i], 0.0)) for i in range(STEPS)]
            for i in range(STEPS):
                inv[i, i] = inv[i, i] - dot(step[i], inv[i, i])
            size *= 2
        inv[0, 1] = -dot(dot(inv[0, 0], lt[0, 1]), inv[1, 1])
        inv[1, 2] = -dot(dot(inv[1, 1], lt[1, 2]), inv[2, 2])
        inv[0, 2] = -dot(dot(inv[0, 0], lt[0, 2]) + dot(inv[0, 1], lt[1, 2]), inv[2, 2])
        zero = jnp.zeros((B, B), jnp.float32)
        for i in range(STEPS):
            for j in range(4):
                litp_ref[pl.ds(4 * i * B + j, B, stride=4), :] = inv.get((i, j), zero)
            for j in range(i, STEPS):
                fac_ref[corner_block("lit", i, j)] = inv[i, j]
            fac_ref[corner_block("li", i, i)] = inv[i, i].T


def gram_kernel(ra_ref, rb_ref, g_ref, fh_ref, fl_ref, litp_ref, pay_ref, y_ref, half_ref, ym_ref, own_ref):
    row, col = lax.axis_index("row"), lax.axis_index("col")
    first = (col // Y_SIZE + row // 4) % 2 == 0
    ra, rb = ra_ref[...], rb_ref[...]
    half_ref[0:48, :] = jnp.where(first, ra, rb)
    half_ref[48:96, :] = jnp.where(first, rb, ra)
    panel = (12 * col + lax.broadcasted_iota(jnp.int32, (12, B), 0)) // B
    top, diag = [], jnp.zeros((12, B), jnp.float32)
    for b in range(8):
        g = g_ref[:, b * B : (b + 1) * B]
        y = g - 2.0 * half_ref[pl.ds(b // 4 * 48 + b % 4, 12, stride=4), :]
        y_ref[b, 0:12, :] = y
        y_ref[b, 12:16, :] = jnp.zeros((4, B), jnp.float32)
        if b < STEPS:
            top.append(y)
            diag = jnp.where(panel == b, g, diag)
            y = jnp.where(row > 0, y, 0.0)
        ym_ref[:, b * B : (b + 1) * B] = y
    yh, yl = split(ym_ref[...])
    fh = fh_ref[...]
    gram = dot_nt(yh, fl_ref[...]) + dot_nt(yl, fh) + dot_nt(yh, fh)
    for k in range(STEPS):
        below = jnp.where(row == 0, top[k], 0.0)
        part = jnp.where(panel >= k, gram[:, k * B : (k + 1) * B], below)
        if k < 2:
            pay_ref[pl.ds(k, 12, stride=2), :] = part
        else:
            pay_ref[24:36, :] = part
    pay_ref[36:48, :] = jnp.where(row == 0, diag, 0.0)
    own_ref[...] = jnp.where(row == 0, litp_ref[pl.ds(pl.multiple_of(48 * col, 16), 48), :], 0.0)
    for k in range(STEPS):
        pay_ref[pl.ds(48 + k, 12, stride=3), :] = own_ref[pl.ds(k, 12, stride=4), :]
    pay_ref[84:88, :] = jnp.zeros((4, B), jnp.float32)


def corner_kernel(mine_ref, other_ref, fac_ref, out_ref, u_ref, vt_ref, wp_ref, cut_ref):
    @pl.when(lax.axis_index("row") == 0)
    def _():
        for x in range(X_SIZE):
            for k in range(4):
                half_ref = mine_ref if k < 2 else other_ref
                u_ref[96 * x : 96 * (x + 1), k * B : (k + 1) * B] = half_ref[
                    pl.ds(192 * x + k % 2, 96, stride=2), :
                ]
        rows = lax.broadcasted_iota(jnp.int32, (B, B), 0)
        cols = lax.broadcasted_iota(jnp.int32, (B, B), 1)

        def blk(i, j):
            return (slice(i * B, (i + 1) * B), slice(j * B, (j + 1) * B))

        def fac(kind, i, j):
            return fac_ref[corner_block(kind, i, j)]

        for j in range(STEPS):
            for k in range(j + 1):
                terms = [dot(fac("lit", j, i), u_ref[blk(i, k)]) for i in range(j, STEPS)]
                vt_ref[blk(j, k)] = functools.reduce(jnp.add, terms)

        def vt(j, k):
            return vt_ref[blk(j, k)]

        def y_of(j, k):
            return u_ref[blk(k, j)].T

        def g_of(k):
            return u_ref[blk(k, STEPS)]

        def diag_adjoint(k, total_t):
            product_t = dot(total_t, fac("l", k, k))
            halved_t = jnp.where(rows < cols, product_t, jnp.where(rows == cols, 0.5 * product_t, 0.0))
            sandwich = dot(dot(fac("lit", k, k), halved_t), fac("li", k, k))
            return 0.5 * (sandwich + sandwich.T)

        l10, l20, l21 = fac("l", 1, 0), fac("l", 2, 0), fac("l", 2, 1)
        li0, li1 = fac("li", 0, 0), fac("li", 1, 1)
        diag2 = diag_adjoint(2, g_of(2) - vt(2, 2))
        off21 = dot(y_of(2, 1) - 2.0 * dot(diag2, l21) - vt(2, 1), li1)
        off12 = off21.T
        diag1 = diag_adjoint(1, g_of(1) - vt(1, 1) - dot(off12, l21))
        off20 = dot(y_of(2, 0) - dot(off21, l10) - 2.0 * dot(diag2, l20) - vt(2, 0), li0)
        off10 = dot(y_of(1, 0) - 2.0 * dot(diag1, l10) - dot(off12, l20) - vt(1, 0), li0)
        off02, off01 = off20.T, off10.T
        diag0 = diag_adjoint(0, g_of(0) - vt(0, 0) - dot(off01, l10) - dot(off02, l20))
        whole = {
            (0, 0): diag0, (1, 1): diag1, (2, 2): diag2,
            (1, 0): 0.5 * off10, (2, 0): 0.5 * off20, (2, 1): 0.5 * off21,
            (0, 1): 0.5 * off01, (0, 2): 0.5 * off02, (1, 2): 0.5 * off12,
        }
        for i in range(STEPS):
            for j in range(STEPS):
                wp_ref[pl.ds(4 * i * B + j, B, stride=4), :] = whole[i, j]
        start = pl.multiple_of(48 * lax.axis_index("col"), 16)
        cut_ref[...] = wp_ref[pl.ds(start, 48), :]
        for k in range(STEPS):
            out_ref[:, k * B : (k + 1) * B] = cut_ref[pl.ds(k, 12, stride=4), :]


def route_kernel(mine_ref, other_ref, out_ref, sum_ref):
    total = mine_ref[...] + other_ref[...]
    sum_ref[...] = total
    out_ref[0] = total[0:40]
    for z in range(1, 8):
        out_ref[z] = total[48:88]


def pack_y_kernel(sum_ref, got_ref, y_ref, out_ref):
    row = lax.axis_index("row")
    corner = sum_ref[0:36, :] + jnp.sum(got_ref[1:, 0:36, :], axis=0)
    inverse = jnp.where(row < 2, sum_ref[48:84, :], got_ref[0, 0:36, :])
    first, second = corner[24:36], sum_ref[36:48, :]
    for y in range(Y_SIZE):
        out_ref[y, pl.ds(0, 12, stride=2), :] = first
        out_ref[y, pl.ds(1, 12, stride=2), :] = second
        out_ref[y, 24:60, :] = inverse
        out_ref[y, 60:72, :] = y_ref[y, 0:12, :]

    @pl.when(row % 2 == 0)
    def _():
        for y in range(Y_SIZE):
            out_ref[y, 0:24, :] = corner[0:24]


def pack_x_kernel(near_ref, out_ref):
    for x in range(X_SIZE):
        for y in range(Y_SIZE):
            out_ref[x, 24 * y : 24 * (y + 1), :] = near_ref[y, 0:24, :]
            out_ref[x, 192 + 12 * y : 192 + 12 * (y + 1), :] = near_ref[y, 60:72, :]


def solve_kernel(near_ref, w_ref, out_ref, half_ref, yt_ref, lit_ref):
    for x in range(X_SIZE):
        yt_ref[96 * x : 96 * (x + 1), :] = w_ref[288 * x + 192 : 288 * (x + 1), :]
    for y in range(Y_SIZE):
        for k in range(STEPS):
            lit_ref[12 * y : 12 * (y + 1), k * B : (k + 1) * B] = near_ref[
                y, pl.ds(24 + k, 12, stride=3), :
            ]
    yt_ref[0:96, :] = 0.5 * dot(lit_ref[...], yt_ref[...])
    for y in range(Y_SIZE):
        out_ref[y, 0:12, :] = yt_ref[12 * y : 12 * (y + 1), :]
        out_ref[y, 12:16, :] = jnp.zeros((4, B), jnp.float32)
    for x in range(X_SIZE):
        half_ref[192 * x : 192 * (x + 1), :] = w_ref[288 * x : 288 * x + 192, :]


def output_kernel(x_ref, corner_ref, out_ref):
    for b in range(8):
        out_ref[:, b * B : (b + 1) * B] = x_ref[b, 0:12, :]

    @pl.when(lax.axis_index("row") == 0)
    def _():
        out_ref[:, 0:PW] = corner_ref[...]


def f32(*shape):
    return jax.ShapeDtypeStruct(shape, jnp.float32)


def bf16(*shape):
    return jax.ShapeDtypeStruct(shape, jnp.bfloat16)


def vmem(*shape):
    return pltpu.VMEM(shape, jnp.float32)


def call(kernel, out_shape, *args, scratch=(), flops=0, after=()):
    many = isinstance(out_shape, (list, tuple))
    spec = pl.BlockSpec(memory_space=pltpu.VMEM)
    total = sum(a.size for a in args) * 4
    return pl.pallas_call(
        kernel,
        out_shape=out_shape,
        in_specs=[spec] * len(args) + [pl.BlockSpec(memory_space=pl.ANY)] * len(after),
        out_specs=[spec] * len(out_shape) if many else spec,
        scratch_shapes=list(scratch),
        compiler_params=PARAMS,
        cost_estimate=pl.CostEstimate(flops=flops, bytes_accessed=total, transcendentals=0),
    )(*args, *after)


def spread(value, axis, groups):
    count = len(groups[0])
    copies = jnp.broadcast_to(value[None], (count,) + value.shape)
    return lax.all_to_all(copies, axis, 0, 0, axis_index_groups=groups)


def between_cores(value):
    return lax.ppermute(value, "row", [(r, r ^ 1) for r in range(16)])


def on_device(trail_adj, factor_panels, factor_adj):
    factor = factor_panels.T.reshape(96, B)
    near = spread(factor, "col", Y_GROUPS).reshape(Y_SIZE * 96, B)
    panels = spread(near, "col", X_GROUPS).reshape(PW * 8, B)
    send, keep, panel_high, panel_low, ft_corner = call(
        product_kernel, [f32(768, B), f32(768, B), bf16(PW, 1024), bf16(PW, 1024), f32(PW, PW)], panels,
        scratch=[vmem(PW, 512), vmem(1536, B), vmem(1024, 512), pltpu.SemaphoreType.DMA((4,))],
        after=[trail_adj], flops=12 * 1024 * 512 * PW,
    )
    fac, inv_tp = call(
        inverse_kernel, [f32(15 * B, B), f32(1536, B)], ft_corner, flops=12 * 60 * B**3,
    )
    both = call(add_kernel, f32(768, B), keep, between_cores(send), after=[inv_tp]).reshape(8, 96, B)
    pieces = lax.all_to_all(both, "row", 0, 0, axis_index_groups=Z_GROUPS)
    send_a, send_b = call(sum_kernel, [f32(48, B), f32(48, B)], pieces)
    devices = [(r, c) for r in range(16) for c in range(32)]
    to_a = [(r * 32 + c, place(r, c, c % 2)) for r, c in devices]
    to_b = [(r * 32 + c, place(r, c, 1 - c % 2)) for r, c in devices]
    got_a = lax.ppermute(send_a, ("row", "col"), to_a)
    got_b = lax.ppermute(send_b, ("row", "col"), to_b)
    payload, own_y = call(
        gram_kernel, [f32(88, B), f32(8, 16, B)], got_a, got_b, factor_adj.T, panel_high, panel_low, inv_tp,
        scratch=[vmem(96, B), vmem(12, 1024), vmem(48, B)], flops=12 * 12 * 1024 * PW,
    )
    out_u, sum_u = call(
        route_kernel, [f32(8, 40, B), f32(88, B)], payload, between_cores(payload),
    )
    got = lax.all_to_all(out_u, "row", 0, 0, axis_index_groups=Z_GROUPS)
    near = call(pack_y_kernel, f32(8, 72, B), sum_u, got, own_y)
    near = lax.all_to_all(near, "col", 0, 0, axis_index_groups=Y_GROUPS)
    wide = call(pack_x_kernel, f32(4, 288, B), near)
    wide = lax.all_to_all(wide, "col", 0, 0, axis_index_groups=X_GROUPS).reshape(4 * 288, B)
    solved, half = call(
        solve_kernel, [f32(8, 16, B), f32(768, B)], near, wide,
        scratch=[vmem(PW, B), vmem(96, PW)], flops=12 * 96 * B * PW,
    )
    rows_x = lax.all_to_all(solved, "col", 0, 0, axis_index_groups=Y_GROUPS)
    corner = call(
        corner_kernel, f32(12, PW), half, between_cores(half), fac,
        scratch=[vmem(PW, 512), vmem(PW, PW), vmem(1536, B), vmem(48, B)],
    )
    out = call(output_kernel, f32(12, 1024), rows_x, corner)
    return out.T


def solution(mesh):
    in_specs = (P("row", "col"), P("row", "col"), P("row", "col"))
    out_specs = P("row", "col")
    return jax.shard_map(
        on_device, mesh=mesh, in_specs=in_specs, out_specs=out_specs, check_vma=False
    )
```

```python
import functools

import jax
import jax.numpy as jnp
from jax import lax
from jax.experimental import pallas as pl
from jax.experimental.pallas import tpu as pltpu
from jax.sharding import PartitionSpec as P

B = 128
STEPS = 3
PW = STEPS * B
HI = lax.Precision.HIGHEST
X_SIZE, Y_SIZE = 4, 8
Y_GROUPS = [[x * Y_SIZE + y for y in range(Y_SIZE)] for x in range(X_SIZE)]
X_GROUPS = [[x * Y_SIZE + y for x in range(X_SIZE)] for y in range(Y_SIZE)]
Z_GROUPS = [[2 * z + core for z in range(8)] for core in range(2)]
PARAMS = pltpu.CompilerParams(vmem_limit_bytes=48 * 1024 * 1024)


def dot(a, b):
    return jnp.dot(a, b, precision=HI, preferred_element_type=jnp.float32)


def dot_bf16(a, b):
    return jnp.dot(a, b, preferred_element_type=jnp.float32)


def dot_nt(a, b):
    return lax.dot_general(a, b, (((1,), (1,)), ((), ())), preferred_element_type=jnp.float32)


def place(row, col, half):
    x, y = col // Y_SIZE, col % Y_SIZE
    x_to, y_to = (x + 2 * (row % 2) + half) % X_SIZE, (y + row // 2 + 12 - col // 4) % Y_SIZE
    return col // 2 * (X_SIZE * Y_SIZE) + x_to * Y_SIZE + y_to


def split(value):
    high = value.astype(jnp.bfloat16)
    return high, (value - high.astype(jnp.float32)).astype(jnp.bfloat16)


def add_kernel(a_ref, b_ref, _, out_ref):
    out_ref[...] = a_ref[...] + b_ref[...]


def product_kernel(
    f_ref, t_hbm_ref, send_ref, keep_ref, fh_ref, fl_ref, top_ref, acc_ref, cut_ref, t_ref, sems
):
    parts = [pl.ds(256 * q, 256) for q in range(4)]
    copies = [
        pltpu.make_async_copy(t_hbm_ref.at[part], t_ref.at[part], sems.at[q])
        for q, part in enumerate(parts)
    ]
    for copy in copies:
        copy.start()
    row, col = lax.axis_index("row"), lax.axis_index("col")
    x, y = col // Y_SIZE, col % Y_SIZE
    panel = lax.broadcasted_iota(jnp.int32, (PW, B), 0) // B
    for b in range(8):
        part = f_ref[pl.ds(b, PW, stride=8), :]
        if b < STEPS:
            top_ref[:, b * B : (b + 1) * B] = part
            part = jnp.where((row > 0) | (panel < b), part, 0.0)
        fh_ref[:, b * B : (b + 1) * B], fl_ref[:, b * B : (b + 1) * B] = split(part)
    for q, part in enumerate(parts):
        copies[q].wait()
        fh, fl = fh_ref[:, part], fl_ref[:, part]
        th, tl = split(t_ref[part, :])
        term = dot_bf16(fh, tl) + dot_bf16(fl, th) + dot_bf16(fh, th)
        acc_ref[...] = term if q == 0 else acc_ref[...] + term
    for b in range(4):
        cut_ref[pl.ds(b, PW, stride=4), :] = acc_ref[:, b * B : (b + 1) * B]
    for core, target in ((1 - row % 2, send_ref), (row % 2, keep_ref)):
        for z in range(8):
            for half in range(2):
                x_to, y_to = (x + 2 * core + half) % X_SIZE, (y + z + 12 - col // 4) % Y_SIZE
                first = pl.multiple_of((x_to * Y_SIZE + y_to) * 48, 16)
                target[z * 96 + half * 48 : z * 96 + half * 48 + 48, :] = cut_ref[pl.ds(first, 48), :]


def sum_kernel(s_ref, a_ref, b_ref):
    odd = lax.axis_index("col") % 2 == 1
    low = jnp.sum(s_ref[:, 0:48, :], axis=0)
    high = jnp.sum(s_ref[:, 48:96, :], axis=0)
    a_ref[...] = jnp.where(odd, high, low)
    b_ref[...] = jnp.where(odd, low, high)


def corner_block(kind, i, j):
    lower = {(0, 0): 0, (1, 0): 1, (1, 1): 2, (2, 0): 3, (2, 1): 4, (2, 2): 5}
    if kind == "l":
        place = lower[i, j]
    elif kind == "lit":
        place = 6 + lower[j, i]
    else:
        place = 12 + i
    return slice(place * B, (place + 1) * B)


def inverse_kernel(top_ref, fac_ref, litp_ref):
    @pl.when(lax.axis_index("row") == 0)
    def _():
        rows = lax.broadcasted_iota(jnp.int32, (B, B), 0)
        cols = lax.broadcasted_iota(jnp.int32, (B, B), 1)
        lt = {}
        for j in range(STEPS):
            for i in range(j + 1):
                value = top_ref[i * B : (i + 1) * B, j * B : (j + 1) * B]
                lt[i, j] = jnp.where(rows <= cols, value, 0.0) if i == j else value
                fac_ref[corner_block("l", j, i)] = lt[i, j].T
        inv = {}
        for i in range(STEPS):
            inv[i, i] = jnp.where(rows == cols, 1.0 / lt[i, i], 0.0)
        size = 1
        while size < B:
            mask = (rows // (2 * size) == cols // (2 * size)) & (rows // size < cols // size)
            step = [dot(inv[i, i], jnp.where(mask, lt[i, i], 0.0)) for i in range(STEPS)]
            for i in range(STEPS):
                inv[i, i] = inv[i, i] - dot(step[i], inv[i, i])
            size *= 2
        inv[0, 1] = -dot(dot(inv[0, 0], lt[0, 1]), inv[1, 1])
        inv[1, 2] = -dot(dot(inv[1, 1], lt[1, 2]), inv[2, 2])
        inv[0, 2] = -dot(dot(inv[0, 0], lt[0, 2]) + dot(inv[0, 1], lt[1, 2]), inv[2, 2])
        zero = jnp.zeros((B, B), jnp.float32)
        for i in range(STEPS):
            for j in range(4):
                litp_ref[pl.ds(4 * i * B + j, B, stride=4), :] = inv.get((i, j), zero)
            for j in range(i, STEPS):
                fac_ref[corner_block("lit", i, j)] = inv[i, j]
            fac_ref[corner_block("li", i, i)] = inv[i, i].T


def gram_kernel(ra_ref, rb_ref, g_ref, fh_ref, fl_ref, litp_ref, pay_ref, y_ref, half_ref, ym_ref, own_ref):
    row, col = lax.axis_index("row"), lax.axis_index("col")
    first = (col // Y_SIZE + row // 4) % 2 == 0
    ra, rb = ra_ref[...], rb_ref[...]
    half_ref[0:48, :] = jnp.where(first, ra, rb)
    half_ref[48:96, :] = jnp.where(first, rb, ra)
    panel = (12 * col + lax.broadcasted_iota(jnp.int32, (12, B), 0)) // B
    top, diag = [], jnp.zeros((12, B), jnp.float32)
    for b in range(8):
        g = g_ref[:, b * B : (b + 1) * B]
        y = g - 2.0 * half_ref[pl.ds(b // 4 * 48 + b % 4, 12, stride=4), :]
        y_ref[b, 0:12, :] = y
        y_ref[b, 12:16, :] = jnp.zeros((4, B), jnp.float32)
        if b < STEPS:
            top.append(y)
            diag = jnp.where(panel == b, g, diag)
            y = jnp.where(row > 0, y, 0.0)
        ym_ref[:, b * B : (b + 1) * B] = y
    yh, yl = split(ym_ref[...])
    fh = fh_ref[...]
    gram = dot_nt(yh, fl_ref[...]) + dot_nt(yl, fh) + dot_nt(yh, fh)
    for k in range(STEPS):
        below = jnp.where(row == 0, top[k], 0.0)
        part = jnp.where(panel >= k, gram[:, k * B : (k + 1) * B], below)
        if k < 2:
            pay_ref[pl.ds(k, 12, stride=2), :] = part
        else:
            pay_ref[24:36, :] = part
    pay_ref[36:48, :] = jnp.where(row == 0, diag, 0.0)
    own_ref[...] = jnp.where(row == 0, litp_ref[pl.ds(pl.multiple_of(48 * col, 16), 48), :], 0.0)
    for k in range(STEPS):
        pay_ref[pl.ds(48 + k, 12, stride=3), :] = own_ref[pl.ds(k, 12, stride=4), :]
    pay_ref[84:88, :] = jnp.zeros((4, B), jnp.float32)


def corner_kernel(mine_ref, other_ref, fac_ref, out_ref, u_ref, vt_ref, wp_ref, cut_ref):
    @pl.when(lax.axis_index("row") == 0)
    def _():
        for x in range(X_SIZE):
            for k in range(4):
                half_ref = mine_ref if k < 2 else other_ref
                u_ref[96 * x : 96 * (x + 1), k * B : (k + 1) * B] = half_ref[
                    pl.ds(192 * x + k % 2, 96, stride=2), :
                ]
        rows = lax.broadcasted_iota(jnp.int32, (B, B), 0)
        cols = lax.broadcasted_iota(jnp.int32, (B, B), 1)

        def blk(i, j):
            return (slice(i * B, (i + 1) * B), slice(j * B, (j + 1) * B))

        def fac(kind, i, j):
            return fac_ref[corner_block(kind, i, j)]

        for j in range(STEPS):
            for k in range(j + 1):
                terms = [dot(fac("lit", j, i), u_ref[blk(i, k)]) for i in range(j, STEPS)]
                vt_ref[blk(j, k)] = functools.reduce(jnp.add, terms)

        def vt(j, k):
            return vt_ref[blk(j, k)]

        def y_of(j, k):
            return u_ref[blk(k, j)].T

        def g_of(k):
            return u_ref[blk(k, STEPS)]

        def diag_adjoint(k, total_t):
            product_t = dot(total_t, fac("l", k, k))
            halved_t = jnp.where(rows < cols, product_t, jnp.where(rows == cols, 0.5 * product_t, 0.0))
            sandwich = dot(dot(fac("lit", k, k), halved_t), fac("li", k, k))
            return 0.5 * (sandwich + sandwich.T)

        l10, l20, l21 = fac("l", 1, 0), fac("l", 2, 0), fac("l", 2, 1)
        li0, li1 = fac("li", 0, 0), fac("li", 1, 1)
        diag2 = diag_adjoint(2, g_of(2) - vt(2, 2))
        off21 = dot(y_of(2, 1) - 2.0 * dot(diag2, l21) - vt(2, 1), li1)
        off12 = off21.T
        diag1 = diag_adjoint(1, g_of(1) - vt(1, 1) - dot(off12, l21))
        off20 = dot(y_of(2, 0) - dot(off21, l10) - 2.0 * dot(diag2, l20) - vt(2, 0), li0)
        off10 = dot(y_of(1, 0) - 2.0 * dot(diag1, l10) - dot(off12, l20) - vt(1, 0), li0)
        off02, off01 = off20.T, off10.T
        diag0 = diag_adjoint(0, g_of(0) - vt(0, 0) - dot(off01, l10) - dot(off02, l20))
        whole = {
            (0, 0): diag0, (1, 1): diag1, (2, 2): diag2,
            (1, 0): 0.5 * off10, (2, 0): 0.5 * off20, (2, 1): 0.5 * off21,
            (0, 1): 0.5 * off01, (0, 2): 0.5 * off02, (1, 2): 0.5 * off12,
        }
        for i in range(STEPS):
            for j in range(STEPS):
                wp_ref[pl.ds(4 * i * B + j, B, stride=4), :] = whole[i, j]
        start = pl.multiple_of(48 * lax.axis_index("col"), 16)
        cut_ref[...] = wp_ref[pl.ds(start, 48), :]
        for k in range(STEPS):
            out_ref[:, k * B : (k + 1) * B] = cut_ref[pl.ds(k, 12, stride=4), :]


def route_kernel(mine_ref, other_ref, out_ref, sum_ref):
    total = mine_ref[...] + other_ref[...]
    sum_ref[...] = total
    out_ref[0] = total[0:40]
    for z in range(1, 8):
        out_ref[z] = total[48:88]


def pack_y_kernel(sum_ref, got_ref, y_ref, out_ref):
    row = lax.axis_index("row")
    corner = sum_ref[0:36, :] + jnp.sum(got_ref[1:, 0:36, :], axis=0)
    inverse = jnp.where(row < 2, sum_ref[48:84, :], got_ref[0, 0:36, :])
    first, second = corner[24:36], sum_ref[36:48, :]
    for y in range(Y_SIZE):
        out_ref[y, pl.ds(0, 12, stride=2), :] = first
        out_ref[y, pl.ds(1, 12, stride=2), :] = second
        out_ref[y, 24:60, :] = inverse
        out_ref[y, 60:72, :] = y_ref[y, 0:12, :]

    @pl.when(row % 2 == 0)
    def _():
        for y in range(Y_SIZE):
            out_ref[y, 0:24, :] = corner[0:24]


def pack_x_kernel(near_ref, out_ref):
    for x in range(X_SIZE):
        for y in range(Y_SIZE):
            out_ref[x, 24 * y : 24 * (y + 1), :] = near_ref[y, 0:24, :]
            out_ref[x, 192 + 12 * y : 192 + 12 * (y + 1), :] = near_ref[y, 60:72, :]


def solve_kernel(near_ref, w_ref, out_ref, half_ref, yt_ref, lit_ref):
    for x in range(X_SIZE):
        yt_ref[96 * x : 96 * (x + 1), :] = w_ref[288 * x + 192 : 288 * (x + 1), :]
    for y in range(Y_SIZE):
        for k in range(STEPS):
            lit_ref[12 * y : 12 * (y + 1), k * B : (k + 1) * B] = near_ref[
                y, pl.ds(24 + k, 12, stride=3), :
            ]
    yt_ref[0:96, :] = 0.5 * dot(lit_ref[...], yt_ref[...])
    for y in range(Y_SIZE):
        out_ref[y, 0:12, :] = yt_ref[12 * y : 12 * (y + 1), :]
        out_ref[y, 12:16, :] = jnp.zeros((4, B), jnp.float32)
    for x in range(X_SIZE):
        half_ref[192 * x : 192 * (x + 1), :] = w_ref[288 * x : 288 * x + 192, :]


def output_kernel(x_ref, corner_ref, out_ref):
    for b in range(8):
        out_ref[:, b * B : (b + 1) * B] = x_ref[b, 0:12, :]

    @pl.when(lax.axis_index("row") == 0)
    def _():
        out_ref[:, 0:PW] = corner_ref[...]


def f32(*shape):
    return jax.ShapeDtypeStruct(shape, jnp.float32)


def bf16(*shape):
    return jax.ShapeDtypeStruct(shape, jnp.bfloat16)


def vmem(*shape):
    return pltpu.VMEM(shape, jnp.float32)


def call(kernel, out_shape, *args, scratch=(), flops=0, after=()):
    many = isinstance(out_shape, (list, tuple))
    spec = pl.BlockSpec(memory_space=pltpu.VMEM)
    total = sum(a.size for a in args) * 4
    return pl.pallas_call(
        kernel,
        out_shape=out_shape,
        in_specs=[spec] * len(args) + [pl.BlockSpec(memory_space=pl.ANY)] * len(after),
        out_specs=[spec] * len(out_shape) if many else spec,
        scratch_shapes=list(scratch),
        compiler_params=PARAMS,
        cost_estimate=pl.CostEstimate(flops=flops, bytes_accessed=total, transcendentals=0),
    )(*args, *after)


def spread(value, axis, groups):
    count = len(groups[0])
    copies = jnp.broadcast_to(value[None], (count,) + value.shape)
    return lax.all_to_all(copies, axis, 0, 0, axis_index_groups=groups)


def between_cores(value):
    return lax.ppermute(value, "row", [(r, r ^ 1) for r in range(16)])


def on_device(trail_adj, factor_panels, factor_adj):
    factor = factor_panels.T.reshape(96, B)
    near = spread(factor, "col", Y_GROUPS).reshape(Y_SIZE * 96, B)
    panels = spread(near, "col", X_GROUPS).reshape(PW * 8, B)
    send, keep, panel_high, panel_low, ft_corner = call(
        product_kernel, [f32(768, B), f32(768, B), bf16(PW, 1024), bf16(PW, 1024), f32(PW, PW)], panels,
        scratch=[vmem(PW, 512), vmem(1536, B), vmem(1024, 512), pltpu.SemaphoreType.DMA((4,))],
        after=[trail_adj], flops=12 * 1024 * 512 * PW,
    )
    fac, inv_tp = call(
        inverse_kernel, [f32(15 * B, B), f32(1536, B)], ft_corner, flops=12 * 60 * B**3,
    )
    both = call(add_kernel, f32(768, B), keep, between_cores(send), after=[inv_tp]).reshape(8, 96, B)
    pieces = lax.all_to_all(both, "row", 0, 0, axis_index_groups=Z_GROUPS)
    send_a, send_b = call(sum_kernel, [f32(48, B), f32(48, B)], pieces)
    devices = [(r, c) for r in range(16) for c in range(32)]
    to_a = [(r * 32 + c, place(r, c, c % 2)) for r, c in devices]
    to_b = [(r * 32 + c, place(r, c, 1 - c % 2)) for r, c in devices]
    got_a = lax.ppermute(send_a, ("row", "col"), to_a)
    got_b = lax.ppermute(send_b, ("row", "col"), to_b)
    payload, own_y = call(
        gram_kernel, [f32(88, B), f32(8, 16, B)], got_a, got_b, factor_adj.T, panel_high, panel_low, inv_tp,
        scratch=[vmem(96, B), vmem(12, 1024), vmem(48, B)], flops=12 * 12 * 1024 * PW,
    )
    out_u, sum_u = call(
        route_kernel, [f32(8, 40, B), f32(88, B)], payload, between_cores(payload),
    )
    got = lax.all_to_all(out_u, "row", 0, 0, axis_index_groups=Z_GROUPS)
    near = call(pack_y_kernel, f32(8, 72, B), sum_u, got, own_y)
    near = lax.all_to_all(near, "col", 0, 0, axis_index_groups=Y_GROUPS)
    wide = call(pack_x_kernel, f32(4, 288, B), near)
    wide = lax.all_to_all(wide, "col", 0, 0, axis_index_groups=X_GROUPS).reshape(4 * 288, B)
    solved, half = call(
        solve_kernel, [f32(8, 16, B), f32(768, B)], near, wide,
        scratch=[vmem(PW, B), vmem(96, PW)], flops=12 * 96 * B * PW,
    )
    rows_x = lax.all_to_all(solved, "col", 0, 0, axis_index_groups=Y_GROUPS)
    corner = call(
        corner_kernel, f32(12, PW), half, lax.ppermute(half, "row", [(1, 0)]), fac,
        scratch=[vmem(PW, 512), vmem(PW, PW), vmem(1536, B), vmem(48, B)],
    )
    out = call(output_kernel, f32(12, 1024), rows_x, corner)
    return out.T


def solution(mesh):
    in_specs = (P("row", "col"), P("row", "col"), P("row", "col"))
    out_specs = P("row", "col")
    return jax.shard_map(
        on_device, mesh=mesh, in_specs=in_specs, out_specs=out_specs, check_vma=False
    )
```

```python
import functools

import jax
import jax.numpy as jnp
from jax import lax
from jax.experimental import pallas as pl
from jax.experimental.pallas import tpu as pltpu
from jax.sharding import PartitionSpec as P

B = 128
STEPS = 3
PW = STEPS * B
HI = lax.Precision.HIGHEST
X_SIZE, Y_SIZE = 4, 8
Y_GROUPS = [[x * Y_SIZE + y for y in range(Y_SIZE)] for x in range(X_SIZE)]
X_GROUPS = [[x * Y_SIZE + y for x in range(X_SIZE)] for y in range(Y_SIZE)]
Z_GROUPS = [[2 * z + core for z in range(8)] for core in range(2)]
PARAMS = pltpu.CompilerParams(vmem_limit_bytes=48 * 1024 * 1024)


def dot(a, b):
    return jnp.dot(a, b, precision=HI, preferred_element_type=jnp.float32)


def dot_bf16(a, b):
    return jnp.dot(a, b, preferred_element_type=jnp.float32)


def dot_nt(a, b):
    return lax.dot_general(a, b, (((1,), (1,)), ((), ())), preferred_element_type=jnp.float32)


def place(row, col):
    x, y = col // Y_SIZE, col % Y_SIZE
    x_to, y_to = (x + 2 * (row % 2) + y % 2) % X_SIZE, (y // 2 * 2 + row // 2 + 12 - col // 4) % Y_SIZE
    return col // 2 * (X_SIZE * Y_SIZE) + x_to * Y_SIZE + y_to


def split(value):
    high = value.astype(jnp.bfloat16)
    return high, (value - high.astype(jnp.float32)).astype(jnp.bfloat16)


def add_kernel(a_ref, b_ref, _, out_ref):
    out_ref[...] = a_ref[...] + b_ref[...]


def product_kernel(
    f_ref, t_hbm_ref, send_ref, keep_ref, fh_ref, fl_ref, top_ref, acc_ref, cut_ref, t_ref, sems
):
    parts = [pl.ds(256 * q, 256) for q in range(4)]
    copies = [
        pltpu.make_async_copy(t_hbm_ref.at[part], t_ref.at[part], sems.at[q])
        for q, part in enumerate(parts)
    ]
    for copy in copies:
        copy.start()
    row, col = lax.axis_index("row"), lax.axis_index("col")
    x, y = col // Y_SIZE, col % Y_SIZE
    panel = lax.broadcasted_iota(jnp.int32, (PW, B), 0) // B
    for b in range(8):
        part = f_ref[pl.ds(b, PW, stride=8), :]
        if b < STEPS:
            top_ref[:, b * B : (b + 1) * B] = part
            part = jnp.where((row > 0) | (panel < b), part, 0.0)
        fh_ref[:, b * B : (b + 1) * B], fl_ref[:, b * B : (b + 1) * B] = split(part)
    for q, part in enumerate(parts):
        copies[q].wait()
        fh, fl = fh_ref[:, part], fl_ref[:, part]
        th, tl = split(t_ref[part, :])
        term = dot_bf16(fh, tl) + dot_bf16(fl, th) + dot_bf16(fh, th)
        acc_ref[...] = term if q == 0 else acc_ref[...] + term
    for b in range(4):
        cut_ref[pl.ds(b, PW, stride=4), :] = acc_ref[:, b * B : (b + 1) * B]
    for core, target in ((1 - row % 2, send_ref), (row % 2, keep_ref)):
        for z in range(8):
            for half in range(2):
                x_to, y_to = (x + 2 * core + half) % X_SIZE, (y // 2 * 2 + z + 12 - col // 4) % Y_SIZE
                first = pl.multiple_of((x_to * Y_SIZE + y_to) * 48, 16)
                target[z * 96 + half * 48 : z * 96 + half * 48 + 48, :] = cut_ref[pl.ds(first, 48), :]


def sum_kernel(s_ref, keep_ref, swap_ref):
    odd = lax.axis_index("col") % 2 == 1
    low = jnp.sum(s_ref[:, 0:48, :], axis=0)
    high = jnp.sum(s_ref[:, 48:96, :], axis=0)
    keep_ref[...] = jnp.where(odd, high, low)
    swap_ref[...] = jnp.where(odd, low, high)


def join_kernel(keep_ref, got_ref, out_ref):
    odd = lax.axis_index("col") % 2 == 1
    keep, got = keep_ref[...], got_ref[...]
    out_ref[0:48, :] = jnp.where(odd, got, keep)
    out_ref[48:96, :] = jnp.where(odd, keep, got)


def corner_block(kind, i, j):
    lower = {(0, 0): 0, (1, 0): 1, (1, 1): 2, (2, 0): 3, (2, 1): 4, (2, 2): 5}
    if kind == "l":
        place = lower[i, j]
    elif kind == "lit":
        place = 6 + lower[j, i]
    else:
        place = 12 + i
    return slice(place * B, (place + 1) * B)


def inverse_kernel(top_ref, fac_ref, litp_ref):
    @pl.when(lax.axis_index("row") == 0)
    def _():
        rows = lax.broadcasted_iota(jnp.int32, (B, B), 0)
        cols = lax.broadcasted_iota(jnp.int32, (B, B), 1)
        lt = {}
        for j in range(STEPS):
            for i in range(j + 1):
                value = top_ref[i * B : (i + 1) * B, j * B : (j + 1) * B]
                lt[i, j] = jnp.where(rows <= cols, value, 0.0) if i == j else value
                fac_ref[corner_block("l", j, i)] = lt[i, j].T
        inv = {}
        for i in range(STEPS):
            inv[i, i] = jnp.where(rows == cols, 1.0 / lt[i, i], 0.0)
        size = 1
        while size < B:
            mask = (rows // (2 * size) == cols // (2 * size)) & (rows // size < cols // size)
            step = [dot(inv[i, i], jnp.where(mask, lt[i, i], 0.0)) for i in range(STEPS)]
            for i in range(STEPS):
                inv[i, i] = inv[i, i] - dot(step[i], inv[i, i])
            size *= 2
        inv[0, 1] = -dot(dot(inv[0, 0], lt[0, 1]), inv[1, 1])
        inv[1, 2] = -dot(dot(inv[1, 1], lt[1, 2]), inv[2, 2])
        inv[0, 2] = -dot(dot(inv[0, 0], lt[0, 2]) + dot(inv[0, 1], lt[1, 2]), inv[2, 2])
        zero = jnp.zeros((B, B), jnp.float32)
        for i in range(STEPS):
            for j in range(4):
                litp_ref[pl.ds(4 * i * B + j, B, stride=4), :] = inv.get((i, j), zero)
            for j in range(i, STEPS):
                fac_ref[corner_block("lit", i, j)] = inv[i, j]
            fac_ref[corner_block("li", i, i)] = inv[i, i].T


def gram_kernel(tc_ref, g_ref, fh_ref, fl_ref, litp_ref, pay_ref, y_ref, ym_ref, own_ref):
    row, col = lax.axis_index("row"), lax.axis_index("col")
    panel = (12 * col + lax.broadcasted_iota(jnp.int32, (12, B), 0)) // B
    top, diag = [], jnp.zeros((12, B), jnp.float32)
    for b in range(8):
        g = g_ref[:, b * B : (b + 1) * B]
        y = g - 2.0 * tc_ref[pl.ds(b // 4 * 48 + b % 4, 12, stride=4), :]
        y_ref[b, 0:12, :] = y
        y_ref[b, 12:16, :] = jnp.zeros((4, B), jnp.float32)
        if b < STEPS:
            top.append(y)
            diag = jnp.where(panel == b, g, diag)
            y = jnp.where(row > 0, y, 0.0)
        ym_ref[:, b * B : (b + 1) * B] = y
    yh, yl = split(ym_ref[...])
    fh = fh_ref[...]
    gram = dot_nt(yh, fl_ref[...]) + dot_nt(yl, fh) + dot_nt(yh, fh)
    for k in range(STEPS):
        below = jnp.where(row == 0, top[k], 0.0)
        part = jnp.where(panel >= k, gram[:, k * B : (k + 1) * B], below)
        if k < 2:
            pay_ref[pl.ds(k, 12, stride=2), :] = part
        else:
            pay_ref[24:36, :] = part
    pay_ref[36:48, :] = jnp.where(row == 0, diag, 0.0)
    own_ref[...] = jnp.where(row == 0, litp_ref[pl.ds(pl.multiple_of(48 * col, 16), 48), :], 0.0)
    for k in range(STEPS):
        pay_ref[pl.ds(48 + k, 12, stride=3), :] = own_ref[pl.ds(k, 12, stride=4), :]
    pay_ref[84:88, :] = jnp.zeros((4, B), jnp.float32)


def corner_kernel(mine_ref, other_ref, fac_ref, out_ref, u_ref, vt_ref, wp_ref, cut_ref):
    @pl.when(lax.axis_index("row") == 0)
    def _():
        for x in range(X_SIZE):
            for k in range(4):
                half_ref = mine_ref if k < 2 else other_ref
                u_ref[96 * x : 96 * (x + 1), k * B : (k + 1) * B] = half_ref[
                    pl.ds(192 * x + k % 2, 96, stride=2), :
                ]
        rows = lax.broadcasted_iota(jnp.int32, (B, B), 0)
        cols = lax.broadcasted_iota(jnp.int32, (B, B), 1)

        def blk(i, j):
            return (slice(i * B, (i + 1) * B), slice(j * B, (j + 1) * B))

        def fac(kind, i, j):
            return fac_ref[corner_block(kind, i, j)]

        for j in range(STEPS):
            for k in range(j + 1):
                terms = [dot(fac("lit", j, i), u_ref[blk(i, k)]) for i in range(j, STEPS)]
                vt_ref[blk(j, k)] = functools.reduce(jnp.add, terms)

        def vt(j, k):
            return vt_ref[blk(j, k)]

        def y_of(j, k):
            return u_ref[blk(k, j)].T

        def g_of(k):
            return u_ref[blk(k, STEPS)]

        def diag_adjoint(k, total_t):
            product_t = dot(total_t, fac("l", k, k))
            halved_t = jnp.where(rows < cols, product_t, jnp.where(rows == cols, 0.5 * product_t, 0.0))
            sandwich = dot(dot(fac("lit", k, k), halved_t), fac("li", k, k))
            return 0.5 * (sandwich + sandwich.T)

        l10, l20, l21 = fac("l", 1, 0), fac("l", 2, 0), fac("l", 2, 1)
        li0, li1 = fac("li", 0, 0), fac("li", 1, 1)
        diag2 = diag_adjoint(2, g_of(2) - vt(2, 2))
        off21 = dot(y_of(2, 1) - 2.0 * dot(diag2, l21) - vt(2, 1), li1)
        off12 = off21.T
        diag1 = diag_adjoint(1, g_of(1) - vt(1, 1) - dot(off12, l21))
        off20 = dot(y_of(2, 0) - dot(off21, l10) - 2.0 * dot(diag2, l20) - vt(2, 0), li0)
        off10 = dot(y_of(1, 0) - 2.0 * dot(diag1, l10) - dot(off12, l20) - vt(1, 0), li0)
        off02, off01 = off20.T, off10.T
        diag0 = diag_adjoint(0, g_of(0) - vt(0, 0) - dot(off01, l10) - dot(off02, l20))
        whole = {
            (0, 0): diag0, (1, 1): diag1, (2, 2): diag2,
            (1, 0): 0.5 * off10, (2, 0): 0.5 * off20, (2, 1): 0.5 * off21,
            (0, 1): 0.5 * off01, (0, 2): 0.5 * off02, (1, 2): 0.5 * off12,
        }
        for i in range(STEPS):
            for j in range(STEPS):
                wp_ref[pl.ds(4 * i * B + j, B, stride=4), :] = whole[i, j]
        start = pl.multiple_of(48 * lax.axis_index("col"), 16)
        cut_ref[...] = wp_ref[pl.ds(start, 48), :]
        for k in range(STEPS):
            out_ref[:, k * B : (k + 1) * B] = cut_ref[pl.ds(k, 12, stride=4), :]


def route_kernel(mine_ref, other_ref, out_ref, sum_ref):
    total = mine_ref[...] + other_ref[...]
    sum_ref[...] = total
    out_ref[0] = total[0:40]
    for z in range(1, 8):
        out_ref[z] = total[48:88]


def pack_y_kernel(sum_ref, got_ref, y_ref, out_ref):
    row = lax.axis_index("row")
    corner = sum_ref[0:36, :] + jnp.sum(got_ref[1:, 0:36, :], axis=0)
    inverse = jnp.where(row < 2, sum_ref[48:84, :], got_ref[0, 0:36, :])
    first, second = corner[24:36], sum_ref[36:48, :]
    for y in range(Y_SIZE):
        out_ref[y, pl.ds(0, 12, stride=2), :] = first
        out_ref[y, pl.ds(1, 12, stride=2), :] = second
        out_ref[y, 24:60, :] = inverse
        out_ref[y, 60:72, :] = y_ref[y, 0:12, :]

    @pl.when(row % 2 == 0)
    def _():
        for y in range(Y_SIZE):
            out_ref[y, 0:24, :] = corner[0:24]


def pack_x_kernel(near_ref, out_ref):
    for x in range(X_SIZE):
        for y in range(Y_SIZE):
            out_ref[x, 24 * y : 24 * (y + 1), :] = near_ref[y, 0:24, :]
            out_ref[x, 192 + 12 * y : 192 + 12 * (y + 1), :] = near_ref[y, 60:72, :]


def half_kernel(w_ref, _, half_ref):
    for x in range(X_SIZE):
        half_ref[192 * x : 192 * (x + 1), :] = w_ref[288 * x : 288 * x + 192, :]


def solve_kernel(near_ref, w_ref, out_ref, yt_ref, lit_ref):
    for x in range(X_SIZE):
        yt_ref[96 * x : 96 * (x + 1), :] = w_ref[288 * x + 192 : 288 * (x + 1), :]
    for y in range(Y_SIZE):
        for k in range(STEPS):
            lit_ref[12 * y : 12 * (y + 1), k * B : (k + 1) * B] = near_ref[
                y, pl.ds(24 + k, 12, stride=3), :
            ]
    lh, ll = split(lit_ref[...])
    yh, yl = split(yt_ref[...])
    yt_ref[0:96, :] = 0.5 * (dot_bf16(lh, yl) + dot_bf16(ll, yh) + dot_bf16(lh, yh))
    for y in range(Y_SIZE):
        out_ref[y, 0:12, :] = yt_ref[12 * y : 12 * (y + 1), :]
        out_ref[y, 12:16, :] = jnp.zeros((4, B), jnp.float32)


def output_kernel(x_ref, corner_ref, out_ref):
    for b in range(8):
        out_ref[:, b * B : (b + 1) * B] = x_ref[b, 0:12, :]

    @pl.when(lax.axis_index("row") == 0)
    def _():
        out_ref[:, 0:PW] = corner_ref[...]


def f32(*shape):
    return jax.ShapeDtypeStruct(shape, jnp.float32)


def bf16(*shape):
    return jax.ShapeDtypeStruct(shape, jnp.bfloat16)


def vmem(*shape):
    return pltpu.VMEM(shape, jnp.float32)


def call(kernel, out_shape, *args, scratch=(), flops=0, after=()):
    many = isinstance(out_shape, (list, tuple))
    spec = pl.BlockSpec(memory_space=pltpu.VMEM)
    total = sum(a.size for a in args) * 4
    return pl.pallas_call(
        kernel,
        out_shape=out_shape,
        in_specs=[spec] * len(args) + [pl.BlockSpec(memory_space=pl.ANY)] * len(after),
        out_specs=[spec] * len(out_shape) if many else spec,
        scratch_shapes=list(scratch),
        compiler_params=PARAMS,
        cost_estimate=pl.CostEstimate(flops=flops, bytes_accessed=total, transcendentals=0),
    )(*args, *after)


def spread(value, axis, groups):
    count = len(groups[0])
    copies = jnp.broadcast_to(value[None], (count,) + value.shape)
    return lax.all_to_all(copies, axis, 0, 0, axis_index_groups=groups)


def between_cores(value):
    return lax.ppermute(value, "row", [(r, r ^ 1) for r in range(16)])


def on_device(trail_adj, factor_panels, factor_adj):
    factor = factor_panels.T.reshape(96, B)
    near = spread(factor, "col", Y_GROUPS).reshape(Y_SIZE * 96, B)
    panels = spread(near, "col", X_GROUPS).reshape(PW * 8, B)
    send, keep, panel_high, panel_low, ft_corner = call(
        product_kernel, [f32(768, B), f32(768, B), bf16(PW, 1024), bf16(PW, 1024), f32(PW, PW)], panels,
        scratch=[vmem(PW, 512), vmem(1536, B), vmem(1024, 512), pltpu.SemaphoreType.DMA((4,))],
        after=[trail_adj], flops=12 * 1024 * 512 * PW,
    )
    fac, inv_tp = call(
        inverse_kernel, [f32(15 * B, B), f32(1536, B)], ft_corner, flops=12 * 60 * B**3,
    )
    both = call(add_kernel, f32(768, B), keep, between_cores(send), after=[inv_tp]).reshape(8, 96, B)
    pieces = lax.all_to_all(both, "row", 0, 0, axis_index_groups=Z_GROUPS)
    keep, swap = call(sum_kernel, [f32(48, B), f32(48, B)], pieces)
    swapped = lax.ppermute(swap, "col", [(c, c ^ 1) for c in range(32)])
    product = call(join_kernel, f32(96, B), keep, swapped)
    moves = [(r * 32 + c, place(r, c)) for r in range(16) for c in range(32)]
    product = lax.ppermute(product, ("row", "col"), moves)
    payload, own_y = call(
        gram_kernel, [f32(88, B), f32(8, 16, B)], product, factor_adj.T, panel_high, panel_low, inv_tp,
        scratch=[vmem(12, 1024), vmem(48, B)], flops=12 * 12 * 1024 * PW,
    )
    out_u, sum_u = call(
        route_kernel, [f32(8, 40, B), f32(88, B)], payload, between_cores(payload),
    )
    got = lax.all_to_all(out_u, "row", 0, 0, axis_index_groups=Z_GROUPS)
    near = call(pack_y_kernel, f32(8, 72, B), sum_u, got, own_y)
    near = lax.all_to_all(near, "col", 0, 0, axis_index_groups=Y_GROUPS)
    wide = call(pack_x_kernel, f32(4, 288, B), near)
    wide = lax.all_to_all(wide, "col", 0, 0, axis_index_groups=X_GROUPS).reshape(4 * 288, B)
    solved = call(
        solve_kernel, f32(8, 16, B), near, wide,
        scratch=[vmem(PW, B), vmem(96, PW)], flops=12 * 96 * B * PW,
    )
    half = call(half_kernel, f32(768, B), wide, after=[solved], flops=10**10)
    rows_x = lax.all_to_all(solved, "col", 0, 0, axis_index_groups=Y_GROUPS)
    corner = call(
        corner_kernel, f32(12, PW), half, between_cores(half), fac,
        scratch=[vmem(PW, 512), vmem(PW, PW), vmem(1536, B), vmem(48, B)],
    )
    out = call(output_kernel, f32(12, 1024), rows_x, corner)
    return out.T


def solution(mesh):
    in_specs = (P("row", "col"), P("row", "col"), P("row", "col"))
    out_specs = P("row", "col")
    return jax.shard_map(
        on_device, mesh=mesh, in_specs=in_specs, out_specs=out_specs, check_vma=False
    )
```

```python
import functools

import jax
import jax.numpy as jnp
from jax import lax
from jax.experimental import pallas as pl
from jax.experimental.pallas import tpu as pltpu
from jax.sharding import PartitionSpec as P

B = 128
STEPS = 3
PW = STEPS * B
HI = lax.Precision.HIGHEST
X_SIZE, Y_SIZE = 4, 8
Y_GROUPS = [[x * Y_SIZE + y for y in range(Y_SIZE)] for x in range(X_SIZE)]
X_GROUPS = [[x * Y_SIZE + y for x in range(X_SIZE)] for y in range(Y_SIZE)]
Z_GROUPS = [[2 * z + core for z in range(8)] for core in range(2)]
PARAMS = pltpu.CompilerParams(vmem_limit_bytes=48 * 1024 * 1024)


def dot(a, b):
    return jnp.dot(a, b, precision=HI, preferred_element_type=jnp.float32)


def dot_bf16(a, b):
    return jnp.dot(a, b, preferred_element_type=jnp.float32)


def dot_nt(a, b):
    return lax.dot_general(a, b, (((1,), (1,)), ((), ())), preferred_element_type=jnp.float32)


def place(row, col):
    x, y = col // Y_SIZE, col % Y_SIZE
    x_to, y_to = (x + 2 * (row % 2) + y % 2) % X_SIZE, (y // 2 * 2 + row // 2 + 12 - col // 4) % Y_SIZE
    return col // 2 * (X_SIZE * Y_SIZE) + x_to * Y_SIZE + y_to


def split(value):
    high = value.astype(jnp.bfloat16)
    return high, (value - high.astype(jnp.float32)).astype(jnp.bfloat16)


def add_kernel(a_ref, b_ref, _, out_ref):
    out_ref[...] = a_ref[...] + b_ref[...]


def half_product(core, fh_ref, fl_ref, th_ref, tl_ref, target, acc_ref, cut_ref, ready):
    col = lax.axis_index("col")
    x, y = col // Y_SIZE, col % Y_SIZE
    firsts = [pl.multiple_of((x + 2 * core + half) % X_SIZE * 96, 32) for half in range(2)]
    for q in range(4):
        part = pl.ds(256 * q, 256)
        ready(q, part)
        fh = jnp.concatenate([fh_ref[pl.ds(first, 96), part] for first in firsts], axis=0)
        fl = jnp.concatenate([fl_ref[pl.ds(first, 96), part] for first in firsts], axis=0)
        th, tl = th_ref[part, :], tl_ref[part, :]
        term = dot_bf16(fh, tl) + dot_bf16(fl, th) + dot_bf16(fh, th)
        acc_ref[...] = term if q == 0 else acc_ref[...] + term
    for b in range(4):
        cut_ref[pl.ds(b, PW // 2, stride=4), :] = acc_ref[:, b * B : (b + 1) * B]
    for z in range(8):
        for half in range(2):
            y_to = (y // 2 * 2 + z + 12 - col // 4) % Y_SIZE
            first = pl.multiple_of(half * 384 + y_to * 48, 16)
            target[z * 96 + half * 48 : z * 96 + half * 48 + 48, :] = cut_ref[pl.ds(first, 48), :]


def product_kernel(
    f_ref, t_hbm_ref, send_ref, fh_ref, fl_ref, top_ref, th_ref, tl_ref, acc_ref, cut_ref, t_ref, sems
):
    parts = [pl.ds(256 * q, 256) for q in range(4)]
    copies = [
        pltpu.make_async_copy(t_hbm_ref.at[part], t_ref.at[part], sems.at[q])
        for q, part in enumerate(parts)
    ]
    for copy in copies:
        copy.start()
    row, col = lax.axis_index("row"), lax.axis_index("col")
    x, y = col // Y_SIZE, col % Y_SIZE
    panel = lax.broadcasted_iota(jnp.int32, (PW, B), 0) // B
    for b in range(8):
        part = f_ref[pl.ds(b, PW, stride=8), :]
        if b < STEPS:
            top_ref[:, b * B : (b + 1) * B] = part
            part = jnp.where((row > 0) | (panel < b), part, 0.0)
        fh_ref[:, b * B : (b + 1) * B], fl_ref[:, b * B : (b + 1) * B] = split(part)

    def ready(q, part):
        copies[q].wait()
        th_ref[part, :], tl_ref[part, :] = split(t_ref[part, :])

    half_product(1 - row % 2, fh_ref, fl_ref, th_ref, tl_ref, send_ref, acc_ref, cut_ref, ready)


def keep_kernel(fh_ref, fl_ref, th_ref, tl_ref, keep_ref, acc_ref, cut_ref):
    core = lax.axis_index("row") % 2
    half_product(core, fh_ref, fl_ref, th_ref, tl_ref, keep_ref, acc_ref, cut_ref, lambda q, part: None)


def sum_kernel(s_ref, keep_ref, swap_ref):
    odd = lax.axis_index("col") % 2 == 1
    low = jnp.sum(s_ref[:, 0:48, :], axis=0)
    high = jnp.sum(s_ref[:, 48:96, :], axis=0)
    keep_ref[...] = jnp.where(odd, high, low)
    swap_ref[...] = jnp.where(odd, low, high)


def join_kernel(keep_ref, got_ref, out_ref):
    odd = lax.axis_index("col") % 2 == 1
    keep, got = keep_ref[...], got_ref[...]
    out_ref[0:48, :] = jnp.where(odd, got, keep)
    out_ref[48:96, :] = jnp.where(odd, keep, got)


def corner_block(kind, i, j):
    lower = {(0, 0): 0, (1, 0): 1, (1, 1): 2, (2, 0): 3, (2, 1): 4, (2, 2): 5}
    if kind == "l":
        place = lower[i, j]
    elif kind == "lit":
        place = 6 + lower[j, i]
    else:
        place = 12 + i
    return slice(place * B, (place + 1) * B)


def inverse_kernel(top_ref, fac_ref, litp_ref):
    @pl.when(lax.axis_index("row") == 0)
    def _():
        rows = lax.broadcasted_iota(jnp.int32, (B, B), 0)
        cols = lax.broadcasted_iota(jnp.int32, (B, B), 1)
        lt = {}
        for j in range(STEPS):
            for i in range(j + 1):
                value = top_ref[i * B : (i + 1) * B, j * B : (j + 1) * B]
                lt[i, j] = jnp.where(rows <= cols, value, 0.0) if i == j else value
                fac_ref[corner_block("l", j, i)] = lt[i, j].T
        inv = {}
        for i in range(STEPS):
            inv[i, i] = jnp.where(rows == cols, 1.0 / lt[i, i], 0.0)
        size = 1
        while size < B:
            mask = (rows // (2 * size) == cols // (2 * size)) & (rows // size < cols // size)
            step = [dot(inv[i, i], jnp.where(mask, lt[i, i], 0.0)) for i in range(STEPS)]
            for i in range(STEPS):
                inv[i, i] = inv[i, i] - dot(step[i], inv[i, i])
            size *= 2
        inv[0, 1] = -dot(dot(inv[0, 0], lt[0, 1]), inv[1, 1])
        inv[1, 2] = -dot(dot(inv[1, 1], lt[1, 2]), inv[2, 2])
        inv[0, 2] = -dot(dot(inv[0, 0], lt[0, 2]) + dot(inv[0, 1], lt[1, 2]), inv[2, 2])
        zero = jnp.zeros((B, B), jnp.float32)
        for i in range(STEPS):
            for j in range(4):
                litp_ref[pl.ds(4 * i * B + j, B, stride=4), :] = inv.get((i, j), zero)
            for j in range(i, STEPS):
                fac_ref[corner_block("lit", i, j)] = inv[i, j]
            fac_ref[corner_block("li", i, i)] = inv[i, i].T


def gram_kernel(tc_ref, g_ref, fh_ref, fl_ref, litp_ref, pay_ref, y_ref, ym_ref, own_ref):
    row, col = lax.axis_index("row"), lax.axis_index("col")
    panel = (12 * col + lax.broadcasted_iota(jnp.int32, (12, B), 0)) // B
    top, diag = [], jnp.zeros((12, B), jnp.float32)
    for b in range(8):
        g = g_ref[:, b * B : (b + 1) * B]
        y = g - 2.0 * tc_ref[pl.ds(b // 4 * 48 + b % 4, 12, stride=4), :]
        y_ref[b, 0:12, :] = y
        y_ref[b, 12:16, :] = jnp.zeros((4, B), jnp.float32)
        if b < STEPS:
            top.append(y)
            diag = jnp.where(panel == b, g, diag)
            y = jnp.where(row > 0, y, 0.0)
        ym_ref[:, b * B : (b + 1) * B] = y
    yh, yl = split(ym_ref[...])
    fh = fh_ref[...]
    gram = dot_nt(yh, fl_ref[...]) + dot_nt(yl, fh) + dot_nt(yh, fh)
    for k in range(STEPS):
        below = jnp.where(row == 0, top[k], 0.0)
        part = jnp.where(panel >= k, gram[:, k * B : (k + 1) * B], below)
        if k < 2:
            pay_ref[pl.ds(k, 12, stride=2), :] = part
        else:
            pay_ref[24:36, :] = part
    pay_ref[36:48, :] = jnp.where(row == 0, diag, 0.0)
    own_ref[...] = jnp.where(row == 0, litp_ref[pl.ds(pl.multiple_of(48 * col, 16), 48), :], 0.0)
    for k in range(STEPS):
        pay_ref[pl.ds(48 + k, 12, stride=3), :] = own_ref[pl.ds(k, 12, stride=4), :]
    pay_ref[84:88, :] = jnp.zeros((4, B), jnp.float32)


def corner_kernel(mine_ref, other_ref, fac_ref, out_ref, u_ref, vt_ref, wp_ref, cut_ref):
    @pl.when(lax.axis_index("row") == 0)
    def _():
        for x in range(X_SIZE):
            for k in range(4):
                half_ref = mine_ref if k < 2 else other_ref
                u_ref[96 * x : 96 * (x + 1), k * B : (k + 1) * B] = half_ref[
                    pl.ds(192 * x + k % 2, 96, stride=2), :
                ]
        rows = lax.broadcasted_iota(jnp.int32, (B, B), 0)
        cols = lax.broadcasted_iota(jnp.int32, (B, B), 1)

        def blk(i, j):
            return (slice(i * B, (i + 1) * B), slice(j * B, (j + 1) * B))

        def fac(kind, i, j):
            return fac_ref[corner_block(kind, i, j)]

        for j in range(STEPS):
            for k in range(j + 1):
                terms = [dot(fac("lit", j, i), u_ref[blk(i, k)]) for i in range(j, STEPS)]
                vt_ref[blk(j, k)] = functools.reduce(jnp.add, terms)

        def vt(j, k):
            return vt_ref[blk(j, k)]

        def y_of(j, k):
            return u_ref[blk(k, j)].T

        def g_of(k):
            return u_ref[blk(k, STEPS)]

        def diag_adjoint(k, total_t):
            product_t = dot(total_t, fac("l", k, k))
            halved_t = jnp.where(rows < cols, product_t, jnp.where(rows == cols, 0.5 * product_t, 0.0))
            sandwich = dot(dot(fac("lit", k, k), halved_t), fac("li", k, k))
            return 0.5 * (sandwich + sandwich.T)

        l10, l20, l21 = fac("l", 1, 0), fac("l", 2, 0), fac("l", 2, 1)
        li0, li1 = fac("li", 0, 0), fac("li", 1, 1)
        diag2 = diag_adjoint(2, g_of(2) - vt(2, 2))
        off21 = dot(y_of(2, 1) - 2.0 * dot(diag2, l21) - vt(2, 1), li1)
        off12 = off21.T
        diag1 = diag_adjoint(1, g_of(1) - vt(1, 1) - dot(off12, l21))
        off20 = dot(y_of(2, 0) - dot(off21, l10) - 2.0 * dot(diag2, l20) - vt(2, 0), li0)
        off10 = dot(y_of(1, 0) - 2.0 * dot(diag1, l10) - dot(off12, l20) - vt(1, 0), li0)
        off02, off01 = off20.T, off10.T
        diag0 = diag_adjoint(0, g_of(0) - vt(0, 0) - dot(off01, l10) - dot(off02, l20))
        whole = {
            (0, 0): diag0, (1, 1): diag1, (2, 2): diag2,
            (1, 0): 0.5 * off10, (2, 0): 0.5 * off20, (2, 1): 0.5 * off21,
            (0, 1): 0.5 * off01, (0, 2): 0.5 * off02, (1, 2): 0.5 * off12,
        }
        for i in range(STEPS):
            for j in range(STEPS):
                wp_ref[pl.ds(4 * i * B + j, B, stride=4), :] = whole[i, j]
        start = pl.multiple_of(48 * lax.axis_index("col"), 16)
        cut_ref[...] = wp_ref[pl.ds(start, 48), :]
        for k in range(STEPS):
            out_ref[:, k * B : (k + 1) * B] = cut_ref[pl.ds(k, 12, stride=4), :]


def route_kernel(mine_ref, other_ref, out_ref, sum_ref):
    total = mine_ref[...] + other_ref[...]
    sum_ref[...] = total
    out_ref[0] = total[0:40]
    for z in range(1, 8):
        out_ref[z] = total[48:88]


def pack_y_kernel(sum_ref, got_ref, y_ref, out_ref):
    row = lax.axis_index("row")
    corner = sum_ref[0:36, :] + jnp.sum(got_ref[1:, 0:36, :], axis=0)
    inverse = jnp.where(row < 2, sum_ref[48:84, :], got_ref[0, 0:36, :])
    first, second = corner[24:36], sum_ref[36:48, :]
    for y in range(Y_SIZE):
        out_ref[y, pl.ds(0, 12, stride=2), :] = first
        out_ref[y, pl.ds(1, 12, stride=2), :] = second
        out_ref[y, 24:60, :] = inverse
        out_ref[y, 60:72, :] = y_ref[y, 0:12, :]

    @pl.when(row % 2 == 0)
    def _():
        for y in range(Y_SIZE):
            out_ref[y, 0:24, :] = corner[0:24]


def pack_x_kernel(near_ref, out_ref):
    for x in range(X_SIZE):
        for y in range(Y_SIZE):
            out_ref[x, 24 * y : 24 * (y + 1), :] = near_ref[y, 0:24, :]
            out_ref[x, 192 + 12 * y : 192 + 12 * (y + 1), :] = near_ref[y, 60:72, :]


def half_kernel(w_ref, _, half_ref):
    for x in range(X_SIZE):
        half_ref[192 * x : 192 * (x + 1), :] = w_ref[288 * x : 288 * x + 192, :]


def solve_kernel(near_ref, w_ref, out_ref, yt_ref, lit_ref):
    for x in range(X_SIZE):
        yt_ref[96 * x : 96 * (x + 1), :] = w_ref[288 * x + 192 : 288 * (x + 1), :]
    for y in range(Y_SIZE):
        for k in range(STEPS):
            lit_ref[12 * y : 12 * (y + 1), k * B : (k + 1) * B] = near_ref[
                y, pl.ds(24 + k, 12, stride=3), :
            ]
    lh, ll = split(lit_ref[...])
    yh, yl = split(yt_ref[...])
    yt_ref[0:96, :] = 0.5 * (dot_bf16(lh, yl) + dot_bf16(ll, yh) + dot_bf16(lh, yh))
    for y in range(Y_SIZE):
        out_ref[y, 0:12, :] = yt_ref[12 * y : 12 * (y + 1), :]
        out_ref[y, 12:16, :] = jnp.zeros((4, B), jnp.float32)


def output_kernel(x_ref, corner_ref, out_ref):
    for b in range(8):
        out_ref[:, b * B : (b + 1) * B] = x_ref[b, 0:12, :]

    @pl.when(lax.axis_index("row") == 0)
    def _():
        out_ref[:, 0:PW] = corner_ref[...]


def f32(*shape):
    return jax.ShapeDtypeStruct(shape, jnp.float32)


def bf16(*shape):
    return jax.ShapeDtypeStruct(shape, jnp.bfloat16)


def vmem(*shape):
    return pltpu.VMEM(shape, jnp.float32)


def call(kernel, out_shape, *args, scratch=(), flops=0, after=()):
    many = isinstance(out_shape, (list, tuple))
    spec = pl.BlockSpec(memory_space=pltpu.VMEM)
    total = sum(a.size for a in args) * 4
    return pl.pallas_call(
        kernel,
        out_shape=out_shape,
        in_specs=[spec] * len(args) + [pl.BlockSpec(memory_space=pl.ANY)] * len(after),
        out_specs=[spec] * len(out_shape) if many else spec,
        scratch_shapes=list(scratch),
        compiler_params=PARAMS,
        cost_estimate=pl.CostEstimate(flops=flops, bytes_accessed=total, transcendentals=0),
    )(*args, *after)


def spread(value, axis, groups):
    count = len(groups[0])
    copies = jnp.broadcast_to(value[None], (count,) + value.shape)
    return lax.all_to_all(copies, axis, 0, 0, axis_index_groups=groups)


def between_cores(value):
    return lax.ppermute(value, "row", [(r, r ^ 1) for r in range(16)])


def on_device(trail_adj, factor_panels, factor_adj):
    factor = factor_panels.T.reshape(96, B)
    near = spread(factor, "col", Y_GROUPS).reshape(Y_SIZE * 96, B)
    panels = spread(near, "col", X_GROUPS).reshape(PW * 8, B)
    send, panel_high, panel_low, ft_corner, trail_high, trail_low = call(
        product_kernel,
        [f32(768, B), bf16(PW, 1024), bf16(PW, 1024), f32(PW, PW), bf16(1024, 512), bf16(1024, 512)],
        panels,
        scratch=[vmem(PW // 2, 512), vmem(768, B), vmem(1024, 512), pltpu.SemaphoreType.DMA((4,))],
        after=[trail_adj], flops=6 * 1024 * 512 * PW,
    )
    keep = call(
        keep_kernel, f32(768, B), panel_high, panel_low, trail_high, trail_low,
        scratch=[vmem(PW // 2, 512), vmem(768, B)], flops=6 * 1024 * 512 * PW,
    )
    fac, inv_tp = call(
        inverse_kernel, [f32(15 * B, B), f32(1536, B)], ft_corner, flops=12 * 60 * B**3,
    )
    both = call(add_kernel, f32(768, B), keep, between_cores(send), after=[inv_tp]).reshape(8, 96, B)
    pieces = lax.all_to_all(both, "row", 0, 0, axis_index_groups=Z_GROUPS)
    keep, swap = call(sum_kernel, [f32(48, B), f32(48, B)], pieces)
    swapped = lax.ppermute(swap, "col", [(c, c ^ 1) for c in range(32)])
    product = call(join_kernel, f32(96, B), keep, swapped)
    moves = [(r * 32 + c, place(r, c)) for r in range(16) for c in range(32)]
    product = lax.ppermute(product, ("row", "col"), moves)
    payload, own_y = call(
        gram_kernel, [f32(88, B), f32(8, 16, B)], product, factor_adj.T, panel_high, panel_low, inv_tp,
        scratch=[vmem(12, 1024), vmem(48, B)], flops=12 * 12 * 1024 * PW,
    )
    out_u, sum_u = call(
        route_kernel, [f32(8, 40, B), f32(88, B)], payload, between_cores(payload),
    )
    got = lax.all_to_all(out_u, "row", 0, 0, axis_index_groups=Z_GROUPS)
    near = call(pack_y_kernel, f32(8, 72, B), sum_u, got, own_y)
    near = lax.all_to_all(near, "col", 0, 0, axis_index_groups=Y_GROUPS)
    wide = call(pack_x_kernel, f32(4, 288, B), near)
    wide = lax.all_to_all(wide, "col", 0, 0, axis_index_groups=X_GROUPS).reshape(4 * 288, B)
    solved = call(
        solve_kernel, f32(8, 16, B), near, wide,
        scratch=[vmem(PW, B), vmem(96, PW)], flops=12 * 96 * B * PW,
    )
    half = call(half_kernel, f32(768, B), wide, after=[solved], flops=10**10)
    rows_x = lax.all_to_all(solved, "col", 0, 0, axis_index_groups=Y_GROUPS)
    corner = call(
        corner_kernel, f32(12, PW), half, between_cores(half), fac,
        scratch=[vmem(PW, 512), vmem(PW, PW), vmem(1536, B), vmem(48, B)],
    )
    out = call(output_kernel, f32(12, 1024), rows_x, corner)
    return out.T


def solution(mesh):
    in_specs = (P("row", "col"), P("row", "col"), P("row", "col"))
    out_specs = P("row", "col")
    return jax.shard_map(
        on_device, mesh=mesh, in_specs=in_specs, out_specs=out_specs, check_vma=False
    )
```

```python
import functools

import jax
import jax.numpy as jnp
from jax import lax
from jax.experimental import pallas as pl
from jax.experimental.pallas import tpu as pltpu
from jax.sharding import PartitionSpec as P

B = 128
STEPS = 3
PW = STEPS * B
HI = lax.Precision.HIGHEST
X_SIZE, Y_SIZE = 4, 8
Y_GROUPS = [[x * Y_SIZE + y for y in range(Y_SIZE)] for x in range(X_SIZE)]
X_GROUPS = [[x * Y_SIZE + y for x in range(X_SIZE)] for y in range(Y_SIZE)]
Z_GROUPS = [[2 * z + core for z in range(8)] for core in range(2)]
PARAMS = pltpu.CompilerParams(vmem_limit_bytes=48 * 1024 * 1024)


def dot(a, b):
    return jnp.dot(a, b, precision=HI, preferred_element_type=jnp.float32)


def dot_bf16(a, b):
    return jnp.dot(a, b, preferred_element_type=jnp.float32)


def dot_nt(a, b):
    return lax.dot_general(a, b, (((1,), (1,)), ((), ())), preferred_element_type=jnp.float32)


def place(row, col):
    x, y = col // Y_SIZE, col % Y_SIZE
    x_to, y_to = (x + 2 * (row % 2) + y % 2) % X_SIZE, (y // 2 * 2 + row // 2 + 12 - col // 4) % Y_SIZE
    return col // 2 * (X_SIZE * Y_SIZE) + x_to * Y_SIZE + y_to


def split(value):
    high = value.astype(jnp.bfloat16)
    return high, (value - high.astype(jnp.float32)).astype(jnp.bfloat16)


def add_kernel(a_ref, b_ref, _, out_ref):
    out_ref[...] = a_ref[...] + b_ref[...]


def half_product(core, fh_ref, fl_ref, th_ref, tl_ref, target, acc_ref, cut_ref, ready):
    col = lax.axis_index("col")
    x, y = col // Y_SIZE, col % Y_SIZE
    firsts = [pl.multiple_of((x + 2 * core + half) % X_SIZE * 96, 32) for half in range(2)]
    for q in range(4):
        part = pl.ds(256 * q, 256)
        ready(q, part)
        fh = jnp.concatenate([fh_ref[pl.ds(first, 96), part] for first in firsts], axis=0)
        fl = jnp.concatenate([fl_ref[pl.ds(first, 96), part] for first in firsts], axis=0)
        th, tl = th_ref[part, :], tl_ref[part, :]
        term = dot_bf16(fh, tl) + dot_bf16(fl, th) + dot_bf16(fh, th)
        acc_ref[...] = term if q == 0 else acc_ref[...] + term
    for b in range(4):
        cut_ref[pl.ds(b, PW // 2, stride=4), :] = acc_ref[:, b * B : (b + 1) * B]
    for z in range(8):
        for half in range(2):
            y_to = (y // 2 * 2 + z + 12 - col // 4) % Y_SIZE
            first = pl.multiple_of(half * 384 + y_to * 48, 16)
            target[z * 96 + half * 48 : z * 96 + half * 48 + 48, :] = cut_ref[pl.ds(first, 48), :]


def product_kernel(
    f_ref, t_hbm_ref, send_ref, fh_ref, fl_ref, top_ref, th_ref, tl_ref, acc_ref, cut_ref, t_ref, sems
):
    parts = [pl.ds(256 * q, 256) for q in range(4)]
    copies = [
        pltpu.make_async_copy(t_hbm_ref.at[part], t_ref.at[part], sems.at[q])
        for q, part in enumerate(parts)
    ]
    for copy in copies:
        copy.start()
    row, col = lax.axis_index("row"), lax.axis_index("col")
    x, y = col // Y_SIZE, col % Y_SIZE
    panel = lax.broadcasted_iota(jnp.int32, (PW, B), 0) // B
    for b in range(8):
        part = f_ref[pl.ds(b, PW, stride=8), :]
        if b < STEPS:
            top_ref[:, b * B : (b + 1) * B] = part
            part = jnp.where((row > 0) | (panel < b), part, 0.0)
        fh_ref[:, b * B : (b + 1) * B], fl_ref[:, b * B : (b + 1) * B] = split(part)

    def ready(q, part):
        copies[q].wait()
        th_ref[part, :], tl_ref[part, :] = split(t_ref[part, :])

    half_product(1 - row % 2, fh_ref, fl_ref, th_ref, tl_ref, send_ref, acc_ref, cut_ref, ready)


def keep_kernel(fh_ref, fl_ref, th_ref, tl_ref, keep_ref, acc_ref, cut_ref):
    core = lax.axis_index("row") % 2
    half_product(core, fh_ref, fl_ref, th_ref, tl_ref, keep_ref, acc_ref, cut_ref, lambda q, part: None)


def sum_kernel(s_ref, keep_ref, swap_ref):
    odd = lax.axis_index("col") % 2 == 1
    low = jnp.sum(s_ref[:, 0:48, :], axis=0)
    high = jnp.sum(s_ref[:, 48:96, :], axis=0)
    keep_ref[...] = jnp.where(odd, high, low)
    swap_ref[...] = jnp.where(odd, low, high)


def join_kernel(keep_ref, got_ref, out_ref):
    odd = lax.axis_index("col") % 2 == 1
    keep, got = keep_ref[...], got_ref[...]
    out_ref[0:48, :] = jnp.where(odd, got, keep)
    out_ref[48:96, :] = jnp.where(odd, keep, got)


def corner_block(kind, i, j):
    lower = {(0, 0): 0, (1, 0): 1, (1, 1): 2, (2, 0): 3, (2, 1): 4, (2, 2): 5}
    if kind == "l":
        place = lower[i, j]
    elif kind == "lit":
        place = 6 + lower[j, i]
    else:
        place = 12 + i
    return slice(place * B, (place + 1) * B)


def inverse_kernel(top_ref, fac_ref, litp_ref):
    @pl.when(lax.axis_index("row") == 0)
    def _():
        rows = lax.broadcasted_iota(jnp.int32, (B, B), 0)
        cols = lax.broadcasted_iota(jnp.int32, (B, B), 1)
        lt = {}
        for j in range(STEPS):
            for i in range(j + 1):
                value = top_ref[i * B : (i + 1) * B, j * B : (j + 1) * B]
                lt[i, j] = jnp.where(rows <= cols, value, 0.0) if i == j else value
                fac_ref[corner_block("l", j, i)] = lt[i, j].T
        inv = {}
        for i in range(STEPS):
            inv[i, i] = jnp.where(rows == cols, 1.0 / lt[i, i], 0.0)
        size = 1
        while size < B:
            mask = (rows // (2 * size) == cols // (2 * size)) & (rows // size < cols // size)
            step = [dot(inv[i, i], jnp.where(mask, lt[i, i], 0.0)) for i in range(STEPS)]
            for i in range(STEPS):
                inv[i, i] = inv[i, i] - dot(step[i], inv[i, i])
            size *= 2
        inv[0, 1] = -dot(dot(inv[0, 0], lt[0, 1]), inv[1, 1])
        inv[1, 2] = -dot(dot(inv[1, 1], lt[1, 2]), inv[2, 2])
        inv[0, 2] = -dot(dot(inv[0, 0], lt[0, 2]) + dot(inv[0, 1], lt[1, 2]), inv[2, 2])
        zero = jnp.zeros((B, B), jnp.float32)
        for i in range(STEPS):
            for j in range(4):
                litp_ref[pl.ds(4 * i * B + j, B, stride=4), :] = inv.get((i, j), zero)
            for j in range(i, STEPS):
                fac_ref[corner_block("lit", i, j)] = inv[i, j]
            fac_ref[corner_block("li", i, i)] = inv[i, i].T


def gram_kernel(tc_ref, g_ref, fh_ref, fl_ref, litp_ref, pay_ref, y_ref, ym_ref, own_ref):
    row, col = lax.axis_index("row"), lax.axis_index("col")
    panel = (12 * col + lax.broadcasted_iota(jnp.int32, (12, B), 0)) // B
    top, diag = [], jnp.zeros((12, B), jnp.float32)
    for b in range(8):
        g = g_ref[:, b * B : (b + 1) * B]
        y = g - 2.0 * tc_ref[pl.ds(b // 4 * 48 + b % 4, 12, stride=4), :]
        y_ref[b, 0:12, :] = y
        y_ref[b, 12:16, :] = jnp.zeros((4, B), jnp.float32)
        if b < STEPS:
            top.append(y)
            diag = jnp.where(panel == b, g, diag)
            y = jnp.where(row > 0, y, 0.0)
        ym_ref[:, b * B : (b + 1) * B] = y
    yh, yl = split(ym_ref[...])
    fh = fh_ref[...]
    gram = dot_nt(yh, fl_ref[...]) + dot_nt(yl, fh) + dot_nt(yh, fh)
    for k in range(STEPS):
        below = jnp.where(row == 0, top[k], 0.0)
        part = jnp.where(panel >= k, gram[:, k * B : (k + 1) * B], below)
        if k < 2:
            pay_ref[pl.ds(k, 12, stride=2), :] = part
        else:
            pay_ref[24:36, :] = part
    pay_ref[36:48, :] = jnp.where(row == 0, diag, 0.0)
    own_ref[...] = jnp.where(row == 0, litp_ref[pl.ds(pl.multiple_of(48 * col, 16), 48), :], 0.0)
    for k in range(STEPS):
        pay_ref[pl.ds(48 + k, 12, stride=3), :] = own_ref[pl.ds(k, 12, stride=4), :]
    pay_ref[84:88, :] = jnp.zeros((4, B), jnp.float32)


def corner_kernel(mine_ref, other_ref, fac_ref, out_ref, u_ref, vt_ref, wp_ref, cut_ref):
    @pl.when(lax.axis_index("row") == 0)
    def _():
        for x in range(X_SIZE):
            for k in range(4):
                half_ref = mine_ref if k < 2 else other_ref
                u_ref[96 * x : 96 * (x + 1), k * B : (k + 1) * B] = half_ref[
                    pl.ds(192 * x + k % 2, 96, stride=2), :
                ]
        rows = lax.broadcasted_iota(jnp.int32, (B, B), 0)
        cols = lax.broadcasted_iota(jnp.int32, (B, B), 1)

        def blk(i, j):
            return (slice(i * B, (i + 1) * B), slice(j * B, (j + 1) * B))

        def fac(kind, i, j):
            return fac_ref[corner_block(kind, i, j)]

        for j in range(STEPS):
            for k in range(j + 1):
                terms = [dot(fac("lit", j, i), u_ref[blk(i, k)]) for i in range(j, STEPS)]
                vt_ref[blk(j, k)] = functools.reduce(jnp.add, terms)

        def vt(j, k):
            return vt_ref[blk(j, k)]

        def y_of(j, k):
            return u_ref[blk(k, j)].T

        def g_of(k):
            return u_ref[blk(k, STEPS)]

        def diag_adjoint(k, total_t):
            product_t = dot(total_t, fac("l", k, k))
            halved_t = jnp.where(rows < cols, product_t, jnp.where(rows == cols, 0.5 * product_t, 0.0))
            sandwich = dot(dot(fac("lit", k, k), halved_t), fac("li", k, k))
            return 0.5 * (sandwich + sandwich.T)

        l10, l20, l21 = fac("l", 1, 0), fac("l", 2, 0), fac("l", 2, 1)
        li0, li1 = fac("li", 0, 0), fac("li", 1, 1)
        diag2 = diag_adjoint(2, g_of(2) - vt(2, 2))
        off21 = dot(y_of(2, 1) - 2.0 * dot(diag2, l21) - vt(2, 1), li1)
        off12 = off21.T
        diag1 = diag_adjoint(1, g_of(1) - vt(1, 1) - dot(off12, l21))
        off20 = dot(y_of(2, 0) - dot(off21, l10) - 2.0 * dot(diag2, l20) - vt(2, 0), li0)
        off10 = dot(y_of(1, 0) - 2.0 * dot(diag1, l10) - dot(off12, l20) - vt(1, 0), li0)
        off02, off01 = off20.T, off10.T
        diag0 = diag_adjoint(0, g_of(0) - vt(0, 0) - dot(off01, l10) - dot(off02, l20))
        whole = {
            (0, 0): diag0, (1, 1): diag1, (2, 2): diag2,
            (1, 0): 0.5 * off10, (2, 0): 0.5 * off20, (2, 1): 0.5 * off21,
            (0, 1): 0.5 * off01, (0, 2): 0.5 * off02, (1, 2): 0.5 * off12,
        }
        for i in range(STEPS):
            for j in range(STEPS):
                wp_ref[pl.ds(4 * i * B + j, B, stride=4), :] = whole[i, j]
        start = pl.multiple_of(48 * lax.axis_index("col"), 16)
        cut_ref[...] = wp_ref[pl.ds(start, 48), :]
        for k in range(STEPS):
            out_ref[:, k * B : (k + 1) * B] = cut_ref[pl.ds(k, 12, stride=4), :]


def route_kernel(mine_ref, other_ref, out_ref, sum_ref):
    total = mine_ref[...] + other_ref[...]
    sum_ref[...] = total
    out_ref[0] = total[0:40]
    for z in range(1, 8):
        out_ref[z] = total[48:88]


def pack_y_kernel(sum_ref, got_ref, y_ref, out_ref):
    row = lax.axis_index("row")
    corner = sum_ref[0:36, :] + jnp.sum(got_ref[1:, 0:36, :], axis=0)
    inverse = jnp.where(row < 2, sum_ref[48:84, :], got_ref[0, 0:36, :])
    first, second = corner[24:36], sum_ref[36:48, :]
    for y in range(Y_SIZE):
        out_ref[y, pl.ds(0, 12, stride=2), :] = first
        out_ref[y, pl.ds(1, 12, stride=2), :] = second
        out_ref[y, 24:60, :] = inverse
        out_ref[y, 60:72, :] = y_ref[y, 0:12, :]

    @pl.when(row % 2 == 0)
    def _():
        for y in range(Y_SIZE):
            out_ref[y, 0:24, :] = corner[0:24]


def pack_x_kernel(near_ref, out_ref):
    for x in range(X_SIZE):
        for y in range(Y_SIZE):
            out_ref[x, 24 * y : 24 * (y + 1), :] = near_ref[y, 0:24, :]
            out_ref[x, 192 + 12 * y : 192 + 12 * (y + 1), :] = near_ref[y, 60:72, :]


def half_kernel(w_ref, _, half_ref):
    for x in range(X_SIZE):
        half_ref[192 * x : 192 * (x + 1), :] = w_ref[288 * x : 288 * x + 192, :]


def solve_kernel(near_ref, w_ref, out_ref, yt_ref, lit_ref):
    for x in range(X_SIZE):
        yt_ref[96 * x : 96 * (x + 1), :] = w_ref[288 * x + 192 : 288 * (x + 1), :]
    for y in range(Y_SIZE):
        for k in range(STEPS):
            lit_ref[12 * y : 12 * (y + 1), k * B : (k + 1) * B] = near_ref[
                y, pl.ds(24 + k, 12, stride=3), :
            ]
    lh, ll = split(lit_ref[...])
    yh, yl = split(yt_ref[...])
    yt_ref[0:96, :] = 0.5 * (dot_bf16(lh, yl) + dot_bf16(ll, yh) + dot_bf16(lh, yh))
    for y in range(Y_SIZE):
        out_ref[y, 0:12, :] = yt_ref[12 * y : 12 * (y + 1), :]
        out_ref[y, 12:16, :] = jnp.zeros((4, B), jnp.float32)


def output_kernel(x_ref, corner_ref, out_ref):
    for b in range(8):
        out_ref[:, b * B : (b + 1) * B] = x_ref[b, 0:12, :]

    @pl.when(lax.axis_index("row") == 0)
    def _():
        out_ref[:, 0:PW] = corner_ref[...]


def f32(*shape):
    return jax.ShapeDtypeStruct(shape, jnp.float32)


def bf16(*shape):
    return jax.ShapeDtypeStruct(shape, jnp.bfloat16)


def vmem(*shape):
    return pltpu.VMEM(shape, jnp.float32)


def call(kernel, out_shape, *args, scratch=(), flops=0, after=()):
    many = isinstance(out_shape, (list, tuple))
    spec = pl.BlockSpec(memory_space=pltpu.VMEM)
    total = sum(a.size for a in args) * 4
    return pl.pallas_call(
        kernel,
        out_shape=out_shape,
        in_specs=[spec] * len(args) + [pl.BlockSpec(memory_space=pl.ANY)] * len(after),
        out_specs=[spec] * len(out_shape) if many else spec,
        scratch_shapes=list(scratch),
        compiler_params=PARAMS,
        cost_estimate=pl.CostEstimate(flops=flops, bytes_accessed=total, transcendentals=0),
    )(*args, *after)


def spread(value, axis, groups):
    count = len(groups[0])
    copies = jnp.broadcast_to(value[None], (count,) + value.shape)
    return lax.all_to_all(copies, axis, 0, 0, axis_index_groups=groups)


def between_cores(value):
    return lax.ppermute(value, "row", [(r, r ^ 1) for r in range(16)])


def on_device(trail_adj, factor_panels, factor_adj):
    factor = factor_panels.T.reshape(96, B)
    near = spread(factor, "col", Y_GROUPS).reshape(Y_SIZE * 96, B)
    panels = spread(near, "col", X_GROUPS).reshape(PW * 8, B)
    send, panel_high, panel_low, ft_corner, trail_high, trail_low = call(
        product_kernel,
        [f32(768, B), bf16(PW, 1024), bf16(PW, 1024), f32(PW, PW), bf16(1024, 512), bf16(1024, 512)],
        panels,
        scratch=[vmem(PW // 2, 512), vmem(768, B), vmem(1024, 512), pltpu.SemaphoreType.DMA((4,))],
        after=[trail_adj], flops=6 * 1024 * 512 * PW,
    )
    keep = call(
        keep_kernel, f32(768, B), panel_high, panel_low, trail_high, trail_low,
        scratch=[vmem(PW // 2, 512), vmem(768, B)], flops=6 * 1024 * 512 * PW,
    )
    fac, inv_tp = call(
        inverse_kernel, [f32(15 * B, B), f32(1536, B)], ft_corner, flops=12 * 60 * B**3,
    )
    both = call(add_kernel, f32(768, B), keep, between_cores(send), after=[inv_tp]).reshape(8, 96, B)
    pieces = lax.all_to_all(both, "row", 0, 0, axis_index_groups=Z_GROUPS)
    keep, swap = call(sum_kernel, [f32(48, B), f32(48, B)], pieces)
    swapped = lax.ppermute(swap, "col", [(c, c ^ 1) for c in range(32)])
    product = call(join_kernel, f32(96, B), keep, swapped)
    moves = [(r * 32 + c, place(r, c)) for r in range(16) for c in range(32)]
    product = lax.ppermute(product, ("row", "col"), moves)
    payload, own_y = call(
        gram_kernel, [f32(88, B), f32(8, 16, B)], product, factor_adj.T, panel_high, panel_low, inv_tp,
        scratch=[vmem(12, 1024), vmem(48, B)], flops=12 * 12 * 1024 * PW,
    )
    out_u, sum_u = call(
        route_kernel, [f32(8, 40, B), f32(88, B)], payload, between_cores(payload),
    )
    got = lax.all_to_all(out_u, "row", 0, 0, axis_index_groups=Z_GROUPS)
    near = call(pack_y_kernel, f32(8, 72, B), sum_u, got, own_y)
    near = lax.all_to_all(near, "col", 0, 0, axis_index_groups=Y_GROUPS)
    wide = call(pack_x_kernel, f32(4, 288, B), near)
    wide = lax.all_to_all(wide, "col", 0, 0, axis_index_groups=X_GROUPS).reshape(4 * 288, B)
    solved = call(
        solve_kernel, f32(8, 16, B), near, wide,
        scratch=[vmem(PW, B), vmem(96, PW)], flops=12 * 96 * B * PW,
    )
    half = call(half_kernel, f32(768, B), wide, after=[solved], flops=10**10)
    rows_x = lax.all_to_all(solved, "col", 0, 0, axis_index_groups=Y_GROUPS)
    corner = call(
        corner_kernel, f32(12, PW), half, lax.ppermute(half, "row", [(1, 0)]), fac,
        scratch=[vmem(PW, 512), vmem(PW, PW), vmem(1536, B), vmem(48, B)],
    )
    out = call(output_kernel, f32(12, 1024), rows_x, corner)
    return out.T


def solution(mesh):
    in_specs = (P("row", "col"), P("row", "col"), P("row", "col"))
    out_specs = P("row", "col")
    return jax.shard_map(
        on_device, mesh=mesh, in_specs=in_specs, out_specs=out_specs, check_vma=False
    )
```
